128 devices in a mesh: shard: 4 (over x), context: 8 (over z_hi, y), tensor: 4 (over z_lo, core).
Axes of the slice: x: 4, y: 4, z: 4 (z_hi: 2, z_lo: 2; z = z_hi * 2 + z_lo), core: 2. Of those that a mesh axis runs over, the one named last changes fastest.
Arguments:
- block_input: bfloat16 [8, 2048, 1152], P('shard', 'context'), may hold values from -6 to 6
- positions: int32 [8, 2048], P('shard', 'context'), may hold values from 0 to 1023, as said below
- cotangent: bfloat16 [8, 2048, 1152], P('shard', 'context'), may hold values from -6 to 6
- query_weight: bfloat16 [1152, 1024], P(('shard', 'context'), 'tensor'), may hold values from -0.1875 to 0.1875
- keyval_weight: bfloat16 [1152, 512], P(('shard', 'context', 'tensor')), may hold values from -0.1875 to 0.1875
- output_weight: bfloat16 [1024, 1152], P('tensor', ('shard', 'context')), may hold values from -0.1875 to 0.1875
- gateup_weight: bfloat16 [1152, 2, 6912], P(('shard', 'context'), None, 'tensor'), may hold values from -0.1875 to 0.1875
- down_weight: bfloat16 [6912, 1152], P('tensor', ('shard', 'context')), may hold values from -0.078125 to 0.078125
- norm_gains: bfloat16 [5120], P(('shard', 'context', 'tensor')), may hold values from 0.099609375 to 1.8984375
- query_first: float32 [1152, 1024], P(('shard', 'context'), 'tensor'), may hold values from -768 to 768
- query_second: float32 [1152, 1024], P(('shard', 'context'), 'tensor'), may hold values from 16384 to 65536
- keyval_first: float32 [1152, 512], P(('shard', 'context', 'tensor')), may hold values from -768 to 768
- keyval_second: float32 [1152, 512], P(('shard', 'context', 'tensor')), may hold values from 16384 to 65536
- output_first: float32 [1024, 1152], P('tensor', ('shard', 'context')), may hold values from -768 to 768
- output_second: float32 [1024, 1152], P('tensor', ('shard', 'context')), may hold values from 16384 to 65536
- gateup_first: float32 [1152, 2, 6912], P(('shard', 'context'), None, 'tensor'), may hold values from -768 to 768
- gateup_second: float32 [1152, 2, 6912], P(('shard', 'context'), None, 'tensor'), may hold values from 16384 to 65536
- down_first: float32 [6912, 1152], P('tensor', ('shard', 'context')), may hold values from -768 to 768
- down_second: float32 [6912, 1152], P('tensor', ('shard', 'context')), may hold values from 16384 to 65536
- gains_first: float32 [5120], P(('shard', 'context', 'tensor')), may hold values from -768 to 768
- gains_second: float32 [5120], P(('shard', 'context', 'tensor')), may hold values from 16384 to 65536
Outputs:
- block_output: bfloat16 [8, 2048, 1152], P('shard', 'context')
- input_grad: float32 [8, 2048, 1152], P('shard', 'context')
- query_grad: float32 [1152, 1024], P(('shard', 'context'), 'tensor')
- query_first_new: float32 [1152, 1024], P(('shard', 'context'), 'tensor')
- query_second_new: float32 [1152, 1024], P(('shard', 'context'), 'tensor')
- query_new: float32 [1152, 1024], P(('shard', 'context'), 'tensor')
- keyval_grad: float32 [1152, 512], P(('shard', 'context', 'tensor'))
- keyval_first_new: float32 [1152, 512], P(('shard', 'context', 'tensor'))
- keyval_second_new: float32 [1152, 512], P(('shard', 'context', 'tensor'))
- keyval_new: float32 [1152, 512], P(('shard', 'context', 'tensor'))
- output_grad: float32 [1024, 1152], P('tensor', ('shard', 'context'))
- output_first_new: float32 [1024, 1152], P('tensor', ('shard', 'context'))
- output_second_new: float32 [1024, 1152], P('tensor', ('shard', 'context'))
- output_new: float32 [1024, 1152], P('tensor', ('shard', 'context'))
- gateup_grad: float32 [1152, 2, 6912], P(('shard', 'context'), None, 'tensor')
- gateup_first_new: float32 [1152, 2, 6912], P(('shard', 'context'), None, 'tensor')
- gateup_second_new: float32 [1152, 2, 6912], P(('shard', 'context'), None, 'tensor')
- gateup_new: float32 [1152, 2, 6912], P(('shard', 'context'), None, 'tensor')
- down_grad: float32 [6912, 1152], P('tensor', ('shard', 'context'))
- down_first_new: float32 [6912, 1152], P('tensor', ('shard', 'context'))
- down_second_new: float32 [6912, 1152], P('tensor', ('shard', 'context'))
- down_new: float32 [6912, 1152], P('tensor', ('shard', 'context'))
- gains_grad: float32 [5120], P(('shard', 'context', 'tensor'))
- gains_first_new: float32 [5120], P(('shard', 'context', 'tensor'))
- gains_second_new: float32 [5120], P(('shard', 'context', 'tensor'))
- gains_new: float32 [5120], P(('shard', 'context', 'tensor'))
The draws below stay inside these ranges and needn't reach their ends.
Inputs may be any that keep to these rules, and one draw needn't show every extreme that they name: `positions`: each sequence is a pack of documents; a token's position counts the tokens before it in its own document, so it is 0 at a document's first token and at the sequence's first token, and rises by one along a document. Every sequence holds one document of exactly 1024 tokens and none longer.
All inputs are finite; a program needn't handle non-finite values.
Results may differ from the reference program's by a relative error of at most 0.035.
Values may be sent and summed in bfloat16 or wider, within the bound.
No kernel may reach another device: no remote copies, remote signals or barrier semaphores. Data moves between devices by JAX's collectives and lax.ppermute only.
A program may use at most 192 MiB of HBM per device.

```python
import math
import jax
import jax.numpy as jnp
from jax import lax

D = 1152
HEADS = 4
HD = 256
FF = 6912
GAINS = 5120
SEQ = 2048
SEQS_ALL = 8
STEP = 4


def draw_positions(key, part):
    start_key, break_key = jax.random.split(key)
    index = jnp.arange(SEQ, dtype=jnp.int32)[None, :]
    long_size = SEQ // 2
    offset = jax.random.randint(start_key, (SEQS_ALL, 1), 0, SEQ - long_size + 1, dtype=jnp.int32)
    spacing = max(SEQ // 8, 2)
    breaks = jax.random.randint(break_key, (SEQS_ALL, SEQ), 0, spacing, dtype=jnp.int32) == 0
    inside = (index > offset) & (index < offset + long_size)
    breaks = breaks & jnp.logical_not(inside) | (index == offset) | (index == offset + long_size) | (index == 0)
    starts = lax.cummax(jnp.where(breaks, index, 0), axis=1)
    return (index - starts).astype(jnp.int32)


def shard_levels(stream_key, dims, cuts, low, high):
    factor_of = 1.0
    for dim, blocks in cuts:
        steps = jax.random.uniform(jax.random.fold_in(jax.random.fold_in(stream_key, 6), dim), (blocks,), jnp.float32, low / len(cuts), high / len(cuts))
        factor_of = factor_of * jnp.repeat(jnp.exp(steps), dims[dim] // blocks).reshape((-1,) + (1,) * (len(dims) - 1 - dim))
    return factor_of


def noise(key, shape, scale, bound, cuts=(), kind=jnp.bfloat16):
    values = jax.random.normal(key, shape, jnp.float32) * scale
    if len(cuts) > 0:
        values = shard_levels(key, shape, cuts, -0.22, 0.18) * values
    return jnp.clip(values, min=-bound, max=bound).astype(kind)


def setup_inputs(seed: int = 0) -> dict:
    key_of = jax.random.split(jax.random.key(seed), 22)
    block_input = noise(key_of[0], (SEQS_ALL, SEQ, D), 1.0, 6.0, ((0, 4), (1, 8)))
    positions = draw_positions(jax.random.fold_in(key_of[21], 71), 0)
    cotangent = noise(key_of[2], (SEQS_ALL, SEQ, D), 1.0, 6.0, ((0, 4), (1, 8)))
    query_weight = noise(key_of[3], (D, HEADS * HD), D ** -0.5, 0.1875, ((0, 32), (1, 4)))
    keyval_weight = noise(key_of[4], (D, 2 * HD), D ** -0.5, 0.1875, ((0, 128),))
    output_weight = noise(key_of[5], (HEADS * HD, D), (HEADS * HD) ** -0.5, 0.1875, ((0, 4), (1, 32)))
    gateup_weight = noise(key_of[6], (D, 2, FF), D ** -0.5, 0.1875, ((0, 32), (2, 4)))
    down_weight = noise(key_of[7], (FF, D), FF ** -0.5, 0.078125, ((0, 4), (1, 32)))
    norm_gains = jnp.clip(1.0 + 0.18 * jax.random.normal(key_of[8], (GAINS,), jnp.float32), 0.099609375, 1.8984375).astype(jnp.bfloat16)
    query_first = noise(key_of[9], (D, HEADS * HD), ((SEQS_ALL * SEQ) ** 0.5), 768.0, ((0, 32), (1, 4)), jnp.float32)
    query_second = jnp.clip(jnp.exp(math.log(65536.0) - 1.3862944 * jax.random.uniform(key_of[10], (D, HEADS * HD), jnp.float32) ** shard_levels(key_of[10], (D, HEADS * HD), ((0, 32), (1, 4)), -0.2, 0.2)), 16384.0, 65536.0)
    keyval_first = noise(key_of[11], (D, 2 * HD), ((SEQS_ALL * SEQ) ** 0.5), 768.0, ((0, 128),), jnp.float32)
    keyval_second = jnp.clip(jnp.exp(math.log(65536.0) - 1.3862944 * jax.random.uniform(key_of[12], (D, 2 * HD), jnp.float32) ** shard_levels(key_of[12], (D, 2 * HD), ((0, 128),), -0.2, 0.2)), 16384.0, 65536.0)
    output_first = noise(key_of[13], (HEADS * HD, D), ((SEQS_ALL * SEQ) ** 0.5), 768.0, ((0, 4), (1, 32)), jnp.float32)
    output_second = jnp.clip(jnp.exp(math.log(65536.0) - 1.3862944 * jax.random.uniform(key_of[14], (HEADS * HD, D), jnp.float32) ** shard_levels(key_of[14], (HEADS * HD, D), ((0, 4), (1, 32)), -0.2, 0.2)), 16384.0, 65536.0)
    gateup_first = noise(key_of[15], (D, 2, FF), ((SEQS_ALL * SEQ) ** 0.5), 768.0, ((0, 32), (2, 4)), jnp.float32)
    gateup_second = jnp.clip(jnp.exp(math.log(65536.0) - 1.3862944 * jax.random.uniform(key_of[16], (D, 2, FF), jnp.float32) ** shard_levels(key_of[16], (D, 2, FF), ((0, 32), (2, 4)), -0.2, 0.2)), 16384.0, 65536.0)
    down_first = noise(key_of[17], (FF, D), ((SEQS_ALL * SEQ) ** 0.5), 768.0, ((0, 4), (1, 32)), jnp.float32)
    down_second = jnp.clip(jnp.exp(math.log(65536.0) - 1.3862944 * jax.random.uniform(key_of[18], (FF, D), jnp.float32) ** shard_levels(key_of[18], (FF, D), ((0, 4), (1, 32)), -0.2, 0.2)), 16384.0, 65536.0)
    gains_first = noise(key_of[19], (GAINS,), ((SEQS_ALL * SEQ) ** 0.5), 768.0, ((0, 128),), jnp.float32)
    gains_second = jnp.clip(jnp.exp(math.log(65536.0) - 1.3862944 * jax.random.uniform(key_of[20], (GAINS,), jnp.float32) ** shard_levels(key_of[20], (GAINS,), ((0, 128),), -0.2, 0.2)), 16384.0, 65536.0)
    return dict(block_input=block_input, positions=positions, cotangent=cotangent, query_weight=query_weight, keyval_weight=keyval_weight, output_weight=output_weight, gateup_weight=gateup_weight, down_weight=down_weight, norm_gains=norm_gains, query_first=query_first, query_second=query_second, keyval_first=keyval_first, keyval_second=keyval_second, output_first=output_first, output_second=output_second, gateup_first=gateup_first, gateup_second=gateup_second, down_first=down_first, down_second=down_second, gains_first=gains_first, gains_second=gains_second)


EPSILON = 1e-06
ROPE_BASE = 1000000.0
LEARN_RATE = 0.02
GAIN_RATE = 0.5
WEIGHT_DECAY = 0.1
BETA_ONE = 0.5
BETA_TWO = 0.5
ADAM_EPS = 1e-08
MASKED = -1e+30

@jax.custom_vjp
def low(v):
    return lax.optimization_barrier(v.astype(jnp.bfloat16)).astype(jnp.float32)

@jax.custom_vjp
def low_back(v):
    return v

def low_keep(v):
    return (low(v), None)

def low_pass(kept, grad):
    return (grad,)

def back_keep(v):
    return (v, None)

def back_low(kept, grad):
    return (low(grad),)
low.defvjp(low_keep, low_pass)
low_back.defvjp(back_keep, back_low)

def matmul(left, right):
    return jnp.dot(left, right, precision=lax.Precision.HIGHEST)

def rms_norm(vector, scale_gain):
    return vector * lax.rsqrt(lax.optimization_barrier(jnp.mean(vector * vector, axis=-1, keepdims=True)) + EPSILON) * scale_gain

def rotation(positions, head_size):
    half_size = head_size // 2
    inverse = jnp.exp(jnp.arange(half_size, dtype=jnp.float32) * (-2.0 * jnp.log(ROPE_BASE) / head_size))
    angles = positions.astype(jnp.float32)[..., None] * inverse
    return (jnp.cos(angles), jnp.sin(angles))

def rotate(vector, cosine, sine):
    half_size = vector.shape[-1] // 2
    first_half = vector[..., :half_size]
    second_half = vector[..., half_size:]
    return jnp.concatenate([first_half * cosine - second_half * sine, second_half * cosine + first_half * sine], axis=-1)

def attend(queries, key_rows, value_rows, positions):
    length, head_count, head_size = queries.shape
    block_rows = min(512, length)
    block_count = length // block_rows
    index = jnp.arange(length, dtype=jnp.int32)
    first_key = index - positions.astype(jnp.int32)

    def one_block(pieces):
        query_block, query_index, query_first = pieces
        scores = jnp.einsum('qhd,kd->hqk', query_block, key_rows, precision=lax.Precision.HIGHEST) * head_size ** (-0.5)
        visible = (index[None, :] <= query_index[:, None]) & (index[None, :] >= query_first[:, None])
        scores = low_back(jnp.where(visible[None], scores, MASKED))
        top_score = lax.optimization_barrier(jnp.max(scores, axis=-1, keepdims=True))
        weights = jnp.exp(scores - top_score)
        weights = weights / lax.optimization_barrier(jnp.sum(weights, axis=-1, keepdims=True))
        return jnp.einsum('hqk,kd->qhd', low(weights), value_rows, precision=lax.Precision.HIGHEST)
    result = lax.map(jax.checkpoint(one_block), (queries.reshape(block_count, block_rows, head_count, head_size), index.reshape(block_count, block_rows), first_key.reshape(block_count, block_rows)))
    return result.reshape(length, head_count, head_size)

def layer(params, block_in, positions):
    query_w, keyval_w, output_w, gateup_w, down_w, gains_all = params
    length, width = block_in.shape
    head_size = keyval_w.shape[1] // 2
    head_count = query_w.shape[1] // head_size
    attn_in_gain = gains_all[:width]
    attn_out_gain = gains_all[width:2 * width]
    ffn_in_gain = gains_all[2 * width:3 * width]
    ffn_out_gain = gains_all[3 * width:4 * width]
    query_gain = gains_all[4 * width:4 * width + head_size]
    key_gain = gains_all[4 * width + head_size:]
    cosine, sine = rotation(positions, head_size)
    normed = low(rms_norm(block_in, attn_in_gain))
    query_raw = low_back(matmul(normed, query_w)).reshape(length, head_count, head_size)
    keyval_raw = low_back(matmul(normed, keyval_w))
    queries = low(rotate(rms_norm(query_raw, query_gain), cosine[:, None, :], sine[:, None, :]))
    key_rows = low(rotate(rms_norm(keyval_raw[:, :head_size], key_gain), cosine, sine))
    value_rows = low(keyval_raw[:, head_size:])
    mixed = low_back(low(attend(queries, key_rows, value_rows, positions))).reshape(length, head_count * head_size)
    projected = low_back(matmul(mixed, output_w))
    middle = block_in + rms_norm(projected, attn_out_gain)
    ffn_in = low(rms_norm(middle, ffn_in_gain))
    gate_up = low_back(jnp.einsum('td,dgf->tgf', ffn_in, gateup_w, precision=lax.Precision.HIGHEST))
    hidden = low(jax.nn.gelu(gate_up[:, 0], approximate=True) * gate_up[:, 1])
    down_sum = low_back(matmul(hidden, down_w))
    return middle + rms_norm(down_sum, ffn_out_gain)

def adam_step(weight, gradient, first_old, second_old, decayed):
    first_new = BETA_ONE * first_old + (1.0 - BETA_ONE) * gradient
    second_new = BETA_TWO * second_old + (1.0 - BETA_TWO) * gradient * gradient
    first_hat = first_new / (1.0 - BETA_ONE ** STEP)
    second_hat = second_new / (1.0 - BETA_TWO ** STEP)
    change = first_hat / (jnp.sqrt(second_hat) + ADAM_EPS)
    if decayed:
        change = change + WEIGHT_DECAY * weight
        rate = LEARN_RATE
    else:
        rate = GAIN_RATE
    return (gradient, first_new, second_new, weight - rate * change)

def reference(block_input, positions, cotangent, query_weight, keyval_weight, output_weight, gateup_weight, down_weight, norm_gains, query_first, query_second, keyval_first, keyval_second, output_first, output_second, gateup_first, gateup_second, down_first, down_second, gains_first, gains_second):
    params = tuple((weight.astype(jnp.float32) for weight in (query_weight, keyval_weight, output_weight, gateup_weight, down_weight, norm_gains)))

    def per_sequence(totals, pieces):
        seq_input, seq_positions, seq_cotangent = pieces
        result, pull_back = jax.vjp(lambda weights, inputs: layer(weights, inputs, seq_positions), params, seq_input.astype(jnp.float32))
        weight_grads, input_grads = pull_back(seq_cotangent.astype(jnp.float32))
        totals = jax.tree.map(lambda first_val, second_val: first_val + second_val, totals, weight_grads)
        return (totals, (result.astype(jnp.bfloat16), input_grads))
    zeros = jax.tree.map(jnp.zeros_like, params)
    grads, (block_output, input_grad) = lax.scan(per_sequence, zeros, (block_input, positions, cotangent))
    firsts = (query_first, keyval_first, output_first, gateup_first, down_first, gains_first)
    seconds = (query_second, keyval_second, output_second, gateup_second, down_second, gains_second)
    results = [block_output, input_grad]
    for number in range(6):
        results.extend(adam_step(params[number], grads[number], firsts[number], seconds[number], number < 5))
    return tuple(results)
```

```python
import jax
import jax.numpy as jnp
from jax import lax
from jax.sharding import Mesh
from jax.sharding import PartitionSpec as P

STEP = 4
EPSILON = 1e-06
ROPE_BASE = 1000000.0
LEARN_RATE = 0.02
GAIN_RATE = 0.5
WEIGHT_DECAY = 0.1
BETA_ONE = 0.5
BETA_TWO = 0.5
ADAM_EPS = 1e-08
MASKED = -1e30
BACK = 4

BF = jnp.bfloat16
F32 = jnp.float32


def dot(spec, left, right):
    return jnp.einsum(spec, left, right, preferred_element_type=F32)


def shift(value, axis, step):
    size = 4 if isinstance(axis, tuple) else lax.axis_size(axis)
    return lax.ppermute(value, axis, [(i, (i + step) % size) for i in range(size)])


def flip(value, axis):
    return shift(value, axis, 1)


def ring_gather(value, axis):
    return [value, shift(value, axis, 1), shift(value, axis, -1), shift(value, axis, 2)]


def ring_scatter(parts, axis):
    got = [shift(parts[1], axis, -1), shift(parts[2], axis, 1), shift(parts[3], axis, 2)]
    return parts[0].astype(F32) + got[0].astype(F32) + got[1].astype(F32) + got[2].astype(F32)


def by_bit(bit, mine, theirs):
    first = jnp.where(bit == 0, mine, theirs)
    return jnp.stack([first, jnp.where(bit == 0, theirs, mine)])


DEPTH = ("zh", "zl")


def wide_gather(own):
    four = jnp.stack(ring_gather(own, DEPTH))
    return jnp.concatenate([four, flip(four, "core")])


def wide_scatter(parts):
    got = flip(parts[4:].astype(BF), "core")
    four = parts[:4].astype(F32) + got.astype(F32)
    low = four.astype(BF)
    return ring_scatter([four[0], low[1], low[2], low[3]], DEPTH)


def token_gather(own):
    two = jnp.stack([own, flip(own, "zl")])
    other = flip(two, "core")
    return jnp.stack([two[0], other[0], two[1], other[1]])


def token_scatter(parts):
    low = parts.astype(BF)
    got = flip(jnp.stack([low[1], low[3]]), "core").astype(F32)
    mine = parts[0].astype(F32) + got[0]
    theirs = (parts[2].astype(F32) + got[1]).astype(BF)
    return mine + flip(theirs, "zl").astype(F32)


def exchange(parts):
    got = flip(jnp.stack([parts[1], parts[3]]), "core")
    over = flip(jnp.stack([parts[2], got[1]]), "zl")
    return [parts[0], got[0], over[0], over[1]]


def inverse_rms(vector):
    return lax.rsqrt(jnp.mean(vector * vector, axis=-1, keepdims=True) + EPSILON)


def rms_norm(vector, gain):
    return vector * inverse_rms(vector) * gain


def rms_back(vector, gain, upstream):
    inverse = inverse_rms(vector)
    scaled = upstream * gain
    inner = jnp.mean(scaled * vector, axis=-1, keepdims=True)
    return (
        inverse * (scaled - vector * (inverse * inverse) * inner),
        jnp.sum(upstream * vector * inverse, axis=0),
    )


def rotation(positions, head_size):
    half_size = head_size // 2
    inverse = jnp.exp(
        jnp.arange(half_size, dtype=F32) * (-2.0 * jnp.log(ROPE_BASE) / head_size)
    )
    angles = positions.astype(F32)[..., None] * inverse
    return jnp.cos(angles), jnp.sin(angles)


def rotate(vector, cosine, sine):
    half_size = vector.shape[-1] // 2
    first_half = vector[..., :half_size]
    second_half = vector[..., half_size:]
    return jnp.concatenate(
        [first_half * cosine - second_half * sine, second_half * cosine + first_half * sine],
        axis=-1,
    )


def adam_step(weight, gradient, first_old, second_old, decayed):
    weight_full = weight.astype(F32)
    first_new = BETA_ONE * first_old + (1.0 - BETA_ONE) * gradient
    second_new = BETA_TWO * second_old + (1.0 - BETA_TWO) * gradient * gradient
    first_hat = first_new / (1.0 - BETA_ONE**STEP)
    second_hat = second_new / (1.0 - BETA_TWO**STEP)
    change = first_hat / (jnp.sqrt(second_hat) + ADAM_EPS)
    if decayed:
        change = change + WEIGHT_DECAY * weight_full
        rate = LEARN_RATE
    else:
        rate = GAIN_RATE
    return (gradient, first_new, second_new, weight_full - rate * change)


def ring_place(index, slot):
    offset = jnp.where(slot == 0, 0, jnp.where(slot == 1, 3, jnp.where(slot == 2, 1, 2)))
    return (index + offset) % 4


def attention(queries, keyval, visible, scale):
    head = queries.shape[-1]
    scores = dot("sqh,skh->sqk", queries, keyval[..., :head]) * scale
    scores = jnp.where(visible, scores, MASKED)
    top = jnp.max(scores, axis=-1, keepdims=True)
    lse = top + jnp.log(jnp.sum(jnp.exp(scores - top), axis=-1, keepdims=True))
    probs = jnp.exp(scores - lse)
    return dot("sqk,skh->sqh", probs.astype(BF), keyval[..., head:]).astype(BF), lse


def attention_back(queries, keyval, visible, scale, lse, upstream):
    head = queries.shape[-1]
    scores = dot("sqh,skh->sqk", queries, keyval[..., :head]) * scale
    probs = jnp.exp(jnp.where(visible, scores, MASKED) - lse)
    d_probs = dot("sqh,skh->sqk", upstream, keyval[..., head:])
    inner = jnp.sum(d_probs * probs, axis=-1, keepdims=True)
    d_scores = (probs * (d_probs - inner)).astype(BF)
    d_queries = dot("sqk,skh->sqh", d_scores, keyval[..., :head]) * scale
    d_keys = dot("sqk,sqh->skh", d_scores, queries) * scale
    d_values = dot("sqk,sqh->skh", probs.astype(BF), upstream)
    return d_queries, jnp.concatenate([d_keys, d_values], axis=-1).astype(BF)


def shards(
    block_input,
    positions,
    cotangent,
    query_weight,
    keyval_weight,
    output_weight,
    gateup_weight,
    down_weight,
    norm_gains,
    query_first,
    query_second,
    keyval_first,
    keyval_second,
    output_first,
    output_second,
    gateup_first,
    gateup_second,
    down_first,
    down_second,
    gains_first,
    gains_second,
):
    seqs, rows, width = block_input.shape
    head = keyval_weight.shape[1] // 2
    quarter = rows // 4
    own = seqs * quarter
    tokens = 4 * own
    scale = head ** (-0.5)
    x_at, zh_at, y_at, zl_at, core_at = (
        lax.axis_index(axis) for axis in ("x", "zh", "y", "zl", "core")
    )
    member = zl_at * 2 + core_at
    context_at = zh_at * 4 + y_at
    row_piece = query_weight.shape[0]

    place = lax.broadcasted_iota(jnp.int32, (width, width), 1)
    source_row = lax.broadcasted_iota(jnp.int32, (width, width), 0)
    group = place // (2 * row_piece)
    inner_row = ((place // row_piece) % 2) * 4 * row_piece + place % row_piece
    straight = (source_row == inner_row + ((group // 4) * 8 + group % 4) * row_piece).astype(BF)
    round_block = ring_place(x_at, group % 4) * 8 + ring_place(y_at, group // 4)
    round_order = (source_row == inner_row + round_block * row_piece).astype(BF)

    part = keyval_weight.shape[0]
    gain_piece = norm_gains.shape[0]
    pad = 2 * head - gain_piece
    piece = jnp.concatenate([keyval_weight, jnp.pad(norm_gains, (0, pad)).reshape(1, -1)])
    piece = by_bit(core_at, piece, flip(piece, "core"))
    piece = by_bit(zl_at, piece, flip(piece, "zl"))
    piece = by_bit(zh_at, piece, flip(piece, "zh")).reshape(8, part + 1, 2 * head)
    keyval_rows = piece[:, :part].reshape(8 * part, 2 * head)
    gain_rows = piece[:, part]

    units = down_weight.shape[0]
    half_units = units // 2
    lanes = -(-half_units // 128) * 128
    fill = ((0, 0), (0, lanes - half_units))
    wide_parts = (gateup_weight[:, 0], gateup_weight[:, 1], down_weight.T)
    lower = jnp.concatenate([jnp.pad(w[:, :half_units], fill) for w in wide_parts], axis=1)
    upper = jnp.concatenate([jnp.pad(w[:, half_units:], fill) for w in wide_parts], axis=1)
    narrow = (output_weight.T, query_weight)
    keep = jnp.concatenate((jnp.where(zh_at == 0, lower, upper),) + narrow, axis=1)
    send = jnp.concatenate((jnp.where(zh_at == 0, upper, lower),) + narrow, axis=1)
    bundle = by_bit(zh_at, keep, flip(send, "zh")).reshape(2 * row_piece, -1)
    bundle = lax.optimization_barrier(bundle)
    big = lax.all_gather(bundle[:, : 3 * lanes + head], ("x", "y"), axis=0, tiled=True)
    full_gateup = big[:, : 2 * lanes]
    full_down = big[:, 2 * lanes : 3 * lanes]
    full_output = big[:, 3 * lanes :]
    small = jnp.concatenate(
        [
            jnp.concatenate([bundle[:, 3 * lanes + head :], keyval_rows], axis=1),
            jnp.pad(gain_rows, ((0, 0), (0, head))),
        ]
    )
    small = lax.optimization_barrier(small)
    line = lax.optimization_barrier(jnp.concatenate(ring_gather(small, "x")))
    small = jnp.concatenate(ring_gather(line, "y")).reshape(16, -1, 3 * head)
    full_query_keyval = small[:, : 2 * row_piece].reshape(width, 3 * head)
    full_query, full_keyval = full_query_keyval[:, :head], full_query_keyval[:, head:]
    slot = lax.broadcasted_iota(jnp.int32, (128, 128), 1)
    holder = (
        (ring_place(x_at, (slot // 8) % 4) * 2 + (slot // 4) % 2) * 4
        + ring_place(y_at, slot // 32)
    ) * 4 + slot % 4
    holder = (lax.broadcasted_iota(jnp.int32, (128, 128), 0) == holder).astype(BF)
    gain_rows = small[:, 2 * row_piece :, :128].reshape(128, 128)
    gains_all = dot("ar,rg->ag", holder, gain_rows)[:, :gain_piece].astype(BF).reshape(-1)
    model_gains = gains_all[: 4 * width].reshape(4, width)
    attn_in_gain = dot("gd,de->ge", model_gains[:1], round_order)[0]
    straight_gains = dot("gd,de->ge", model_gains[1:], straight)
    attn_out_gain, ffn_in_gain, ffn_out_gain = (straight_gains[i] for i in range(3))
    query_gain = gains_all[4 * width : 4 * width + head].astype(F32)
    key_gain = gains_all[4 * width + head :].astype(F32)

    starts = [(member ^ k) * quarter for k in range(4)]

    def quarters(array):
        return jnp.stack(
            [lax.dynamic_slice_in_dim(array, start, quarter, 1) for start in starts]
        )

    token_rows = quarters(block_input).reshape(tokens, width)
    inputs = dot("td,de->te", token_rows, round_order)
    own_inputs = dot("td,de->te", token_rows[:own], straight)
    own_cotangent = lax.dynamic_slice_in_dim(cotangent, starts[0], quarter, 1)
    upstream = dot("td,de->te", own_cotangent.reshape(own, width), straight)
    local_row = jnp.stack([start + jnp.arange(quarter, dtype=jnp.int32) for start in starts])
    place_of = quarters(positions)
    cosine, sine = rotation(place_of.reshape(tokens), head)

    normed = rms_norm(inputs, attn_in_gain).astype(BF)
    raw = dot("td,dh->th", normed, full_query_keyval)
    query_raw, key_raw, value_raw = raw[:, :head], raw[:, head : 2 * head], raw[:, 2 * head :]
    queries = rotate(rms_norm(query_raw, query_gain), cosine, sine).astype(BF)
    key_rows = rotate(rms_norm(key_raw, key_gain), cosine, sine)
    keyval = jnp.concatenate([key_rows, value_raw], axis=1).astype(BF)
    keyval = keyval.reshape(4, seqs, quarter, 2 * head)
    half = jnp.stack([keyval[0], keyval[2]])
    got = jnp.stack(
        [
            lax.ppermute(half, ("zh", "y"), [(i, i + back) for i in range(8 - back)])
            for back in range(BACK, 0, -1)
        ]
    )
    other = flip(got, "core")
    blocks = jnp.stack([got[:, 0], other[:, 0], got[:, 1], other[:, 1]], axis=1)
    keys_all = jnp.concatenate([blocks, keyval[None]])
    keys_all = keys_all.transpose(2, 0, 1, 3, 4).reshape(seqs, (BACK + 1) * rows, 2 * head)

    query_index = context_at * rows + local_row
    first_key = query_index[:, None, :] - place_of
    first_key = first_key.transpose(1, 0, 2).reshape(seqs, rows)
    key_index = (context_at + jnp.arange(-BACK, 1, dtype=jnp.int32))[:, None, None] * rows
    key_index = (key_index + local_row[None]).reshape(1, 1, -1)
    visible = (key_index <= query_index.reshape(1, rows, 1)) & (
        key_index >= first_key[:, :, None]
    )

    def by_sequence(array):
        return array.reshape(4, seqs, quarter, -1).transpose(1, 0, 2, 3).reshape(seqs, rows, -1)

    def by_quarter(array):
        return array.reshape(seqs, 4, quarter, -1).transpose(1, 0, 2, 3).reshape(tokens, -1)

    sequence_queries = by_sequence(queries)
    attended, lse = attention(sequence_queries, keys_all, visible, scale)
    attended = by_quarter(attended)
    projected = token_scatter(
        dot("th,dh->td", attended, full_output).reshape(4, own, width)
    )
    middle = own_inputs + rms_norm(projected, attn_out_gain)
    ffn_own = rms_norm(middle, ffn_in_gain).astype(BF)
    ffn_in = wide_gather(ffn_own).reshape(2 * tokens, width)
    gate_up = dot("td,df->tf", ffn_in, full_gateup)

    def geglu(pair):
        return jax.nn.gelu(pair[:, :lanes], approximate=True) * pair[:, lanes:]

    hidden, geglu_back = jax.vjp(geglu, gate_up)
    hidden = hidden.astype(BF)
    down_sum = wide_scatter(dot("tf,df->td", hidden, full_down).reshape(8, own, width))
    own_output = (middle + rms_norm(down_sum, ffn_out_gain)).astype(BF)

    def to_whole(plain):
        parts = token_gather(plain).reshape(4, seqs, quarter, width)
        whole = jnp.zeros((seqs, rows, width), BF)
        for k in range(4):
            whole = lax.dynamic_update_slice_in_dim(whole, parts[k], starts[k], 1)
        return whole

    block_output = to_whole(dot("te,de->td", own_output, straight).astype(BF))

    d_down, grad_ffn_out = rms_back(down_sum, ffn_out_gain, upstream)
    d_down = wide_gather(d_down.astype(BF)).reshape(2 * tokens, width)
    down_term = dot("td,tf->df", d_down, hidden).astype(BF)
    down_rows = lax.psum_scatter(down_term, ("x", "y"), scatter_dimension=0, tiled=True)
    d_hidden = dot("td,df->tf", d_down, full_down)
    d_gateup = geglu_back(d_hidden)[0].astype(BF)
    d_ffn = wide_scatter(dot("tf,df->td", d_gateup, full_gateup).reshape(8, own, width))
    gateup_term = dot("td,tf->df", ffn_in, d_gateup).astype(BF)
    gateup_rows = lax.psum_scatter(gateup_term, ("x", "y"), scatter_dimension=0, tiled=True)
    d_middle, grad_ffn_in = rms_back(middle, ffn_in_gain, d_ffn)
    d_middle = upstream + d_middle
    d_projected, grad_attn_out = rms_back(projected, attn_out_gain, d_middle)
    d_projected = token_gather(d_projected.astype(BF)).reshape(tokens, width)
    output_term = dot("td,th->dh", d_projected, attended).astype(BF)
    d_attended = dot("td,dh->th", d_projected, full_output).astype(BF)
    d_queries, d_keyval = attention_back(
        sequence_queries, keys_all, visible, scale, lse, by_sequence(d_attended)
    )
    d_queries = by_quarter(d_queries)
    d_keyval = d_keyval.reshape(seqs, BACK + 1, 4, quarter, 2 * head).transpose(1, 2, 0, 3, 4)
    got = flip(jnp.stack([d_keyval[:, 1], d_keyval[:, 3]], axis=1), "core")
    halves = jnp.stack([d_keyval[:, 0], d_keyval[:, 2]], axis=1).astype(F32) + got.astype(F32)
    half = halves[BACK]
    for back in range(1, BACK + 1):
        term = lax.ppermute(
            halves[BACK - back].astype(BF),
            ("zh", "y"),
            [(i + back, i) for i in range(8 - back)],
        )
        half = half + term.astype(F32)
    d_keyval = half[0] + flip(half[1].astype(BF), "zl").astype(F32)
    d_keyval = d_keyval.reshape(own, 2 * head)

    def query_path(raw_rows, gain):
        return rotate(rms_norm(raw_rows, gain), cosine, sine)

    def key_path(raw_rows, gain):
        return rotate(rms_norm(raw_rows, gain), cosine[:own], sine[:own])

    unused_query, query_back = jax.vjp(query_path, query_raw, query_gain)
    d_query_raw, grad_query = query_back(d_queries)
    d_query_raw = d_query_raw.astype(BF)
    straight_normed = dot(
        "td,de->te", dot("te,de->td", normed, round_order).astype(BF), straight
    ).astype(BF)
    query_term = dot("td,th->dh", straight_normed, d_query_raw).astype(BF)
    narrow_rows = lax.psum_scatter(
        jnp.concatenate([output_term, query_term], axis=1),
        ("x", "y"),
        scatter_dimension=0,
        tiled=True,
    )
    d_normed_query = dot("th,dh->td", d_query_raw, full_query)
    d_normed = token_scatter(d_normed_query.reshape(4, own, width))
    unused_key, key_back = jax.vjp(key_path, key_raw[:own], key_gain)
    d_key_raw, grad_key = key_back(d_keyval[:, :head])
    d_keyval_raw = jnp.concatenate([d_key_raw, d_keyval[:, head:]], axis=1).astype(BF)
    columns = 2 * head // 4
    column_parts = exchange(
        [
            lax.dynamic_slice_in_dim(d_keyval_raw, (member ^ k) * columns, columns, 1)
            for k in range(4)
        ]
    )
    keyval_term = dot("td,tk->dk", normed, jnp.concatenate(column_parts)).astype(BF)
    d_normed_keyval = dot("tk,dk->td", d_keyval_raw, full_keyval)
    inverse = inverse_rms(inputs)
    grad_attn_in = jnp.sum(d_normed_query * inputs * inverse, axis=0) + jnp.sum(
        d_normed_keyval * inputs[:own] * inverse[:own], axis=0
    )
    d_inputs, unused_gain = rms_back(inputs[:own], attn_in_gain, d_normed + d_normed_keyval)
    input_grad = dot("te,de->td", d_middle.astype(BF), straight) + dot(
        "te,de->td", d_inputs.astype(BF), round_order
    )
    input_grad = to_whole(input_grad.astype(BF)).astype(F32)

    wide = jnp.stack([grad_attn_out, grad_ffn_in, grad_ffn_out]).astype(BF)
    total = jnp.concatenate(
        [
            dot("ge,de->gd", grad_attn_in.astype(BF).reshape(1, -1), round_order).reshape(-1),
            dot("ge,de->gd", wide, straight).reshape(-1),
            grad_query,
            grad_key,
        ]
    )
    total = total.astype(BF).reshape(128, gain_piece)
    total = dot("ar,ag->rg", holder, jnp.pad(total, ((0, 0), (0, columns - gain_piece))))
    terms = jnp.concatenate(
        [keyval_term.reshape(16, -1, columns), total.astype(BF).reshape(16, 8, columns)], axis=1
    )
    terms = ring_scatter([terms[4 * i : 4 * i + 4] for i in range(4)], "y").astype(BF)
    terms = ring_scatter([terms[i] for i in range(4)], "x")
    keyval_part = terms[: 2 * row_piece].reshape(2, 4, part, columns)
    gain_part = terms[2 * row_piece :].reshape(2, 4, 1, columns)
    both = jnp.concatenate([keyval_part, gain_part], axis=2)
    mine = jnp.where(zh_at == 0, both[0], both[1])
    theirs = jnp.where(zh_at == 0, both[1], both[0]).astype(BF)
    mine = mine + flip(theirs, "zh").astype(F32)
    owners = exchange(
        [lax.dynamic_index_in_dim(mine, member ^ k, 0, keepdims=False) for k in range(4)]
    )
    keyval_grad = jnp.zeros((part, 2 * head), F32)
    gains_grad = jnp.zeros((gain_piece,), F32)
    for k in range(4):
        keyval_grad = lax.dynamic_update_slice_in_dim(
            keyval_grad, owners[k][:part], (member ^ k) * columns, 1
        )
        gains_grad = gains_grad + owners[k][part, :gain_piece]

    rows_all = jnp.concatenate([gateup_rows, down_rows], axis=1)
    mine = jnp.where(zh_at == 0, rows_all[:row_piece], rows_all[row_piece:])
    theirs = jnp.where(zh_at == 0, rows_all[row_piece:], rows_all[:row_piece])
    both = by_bit(zh_at, mine, flip(theirs, "zh")).astype(F32)
    gate_grad, up_grad, down_grad = (
        jnp.concatenate(
            [both[i][:, lanes * j : lanes * j + half_units] for i in range(2)], axis=1
        )
        for j in range(3)
    )
    gateup_grad = jnp.stack([gate_grad, up_grad], axis=1)
    down_grad = down_grad.T
    mine = jnp.where(zh_at == 0, narrow_rows[:row_piece], narrow_rows[row_piece:])
    theirs = jnp.where(zh_at == 0, narrow_rows[row_piece:], narrow_rows[:row_piece])
    narrow_grad = mine.astype(F32) + flip(theirs, "zh").astype(F32)
    output_grad = narrow_grad[:, :head].T
    query_grad = narrow_grad[:, head:]

    results = [block_output, input_grad]
    results.extend(adam_step(query_weight, query_grad, query_first, query_second, True))
    results.extend(adam_step(keyval_weight, keyval_grad, keyval_first, keyval_second, True))
    results.extend(adam_step(output_weight, output_grad, output_first, output_second, True))
    results.extend(adam_step(gateup_weight, gateup_grad, gateup_first, gateup_second, True))
    results.extend(adam_step(down_weight, down_grad, down_first, down_second, True))
    results.extend(adam_step(norm_gains, gains_grad, gains_first, gains_second, False))
    return tuple(results)


def solution(mesh):
    fine = Mesh(mesh.devices.reshape(4, 2, 4, 2, 2), ("x", "zh", "y", "zl", "core"))
    context = ("zh", "y")
    tensor = ("zl", "core")
    fsdp = ("x", "zh", "y")
    everything = fsdp + tensor
    stream = P("x", context, None)
    query = P(fsdp, tensor)
    keyval = P(everything, None)
    output = P(tensor, fsdp)
    gateup = P(fsdp, None, tensor)
    gains = P(everything)
    return jax.shard_map(
        shards,
        mesh=fine,
        in_specs=(
            stream, P("x", context), stream,
            query, keyval, output, gateup, output, gains,
            query, query, keyval, keyval, output, output,
            gateup, gateup, output, output, gains, gains,
        ),
        out_specs=(stream, stream)
        + (query,) * 4
        + (keyval,) * 4
        + (output,) * 4
        + (gateup,) * 4
        + (output,) * 4
        + (gains,) * 4,
        check_vma=False,
    )
```

```python
import jax
import jax.numpy as jnp
from jax import lax
from jax.sharding import Mesh
from jax.sharding import PartitionSpec as P

STEP = 4
EPSILON = 1e-06
ROPE_BASE = 1000000.0
LEARN_RATE = 0.02
GAIN_RATE = 0.5
WEIGHT_DECAY = 0.1
BETA_ONE = 0.5
BETA_TWO = 0.5
ADAM_EPS = 1e-08
MASKED = -1e30
BACK = 4

BF = jnp.bfloat16
F32 = jnp.float32


def dot(spec, left, right):
    return jnp.einsum(spec, left, right, preferred_element_type=F32)


def shift(value, axis, step):
    size = 4 if isinstance(axis, tuple) else lax.axis_size(axis)
    return lax.ppermute(value, axis, [(i, (i + step) % size) for i in range(size)])


def flip(value, axis):
    return shift(value, axis, 1)


def ring_gather(value, axis):
    return [value, shift(value, axis, 1), shift(value, axis, -1), shift(value, axis, 2)]


def ring_scatter(parts, axis):
    got = [shift(parts[1], axis, -1), shift(parts[2], axis, 1), shift(parts[3], axis, 2)]
    return parts[0].astype(F32) + got[0].astype(F32) + got[1].astype(F32) + got[2].astype(F32)


def by_bit(bit, mine, theirs):
    first = jnp.where(bit == 0, mine, theirs)
    return jnp.stack([first, jnp.where(bit == 0, theirs, mine)])


DEPTH = ("zh", "zl")


def wide_gather(own):
    four = jnp.stack(ring_gather(own, DEPTH))
    return jnp.concatenate([four, flip(four, "core")])


def wide_scatter(parts):
    got = flip(parts[4:].astype(BF), "core")
    four = parts[:4].astype(F32) + got.astype(F32)
    low = four.astype(BF)
    return ring_scatter([four[0], low[1], low[2], low[3]], DEPTH)


def token_gather(own):
    two = jnp.stack([own, flip(own, "zl")], axis=1)
    other = flip(two, "core")
    return jnp.stack([two[:, 0], other[:, 0], two[:, 1], other[:, 1]], axis=1)


def token_scatter(parts):
    got = flip(parts[:, 1::2].astype(BF), "core").astype(F32)
    mine = parts[:, 0].astype(F32) + got[:, 0]
    theirs = (parts[:, 2].astype(F32) + got[:, 1]).astype(BF)
    return mine + flip(theirs, "zl").astype(F32)


def exchange(parts):
    got = flip(jnp.stack([parts[1], parts[3]]), "core")
    over = flip(jnp.stack([parts[2], got[1]]), "zl")
    return [parts[0], got[0], over[0], over[1]]


def inverse_rms(vector):
    return lax.rsqrt(jnp.mean(vector * vector, axis=-1, keepdims=True) + EPSILON)


def rms_norm(vector, gain):
    return vector * inverse_rms(vector) * gain


def rms_back(vector, gain, upstream):
    inverse = inverse_rms(vector)
    scaled = upstream * gain
    inner = jnp.mean(scaled * vector, axis=-1, keepdims=True)
    return (
        inverse * (scaled - vector * (inverse * inverse) * inner),
        jnp.sum(upstream * vector * inverse, axis=0),
    )


def rotation(positions, head_size):
    half_size = head_size // 2
    inverse = jnp.exp(
        jnp.arange(half_size, dtype=F32) * (-2.0 * jnp.log(ROPE_BASE) / head_size)
    )
    angles = positions.astype(F32)[..., None] * inverse
    return jnp.cos(angles), jnp.sin(angles)


def rotate(vector, cosine, sine):
    half_size = vector.shape[-1] // 2
    first_half = vector[..., :half_size]
    second_half = vector[..., half_size:]
    return jnp.concatenate(
        [first_half * cosine - second_half * sine, second_half * cosine + first_half * sine],
        axis=-1,
    )


def adam_step(weight, gradient, first_old, second_old, decayed):
    weight_full = weight.astype(F32)
    first_new = BETA_ONE * first_old + (1.0 - BETA_ONE) * gradient
    second_new = BETA_TWO * second_old + (1.0 - BETA_TWO) * gradient * gradient
    first_hat = first_new / (1.0 - BETA_ONE**STEP)
    second_hat = second_new / (1.0 - BETA_TWO**STEP)
    change = first_hat / (jnp.sqrt(second_hat) + ADAM_EPS)
    if decayed:
        change = change + WEIGHT_DECAY * weight_full
        rate = LEARN_RATE
    else:
        rate = GAIN_RATE
    return (gradient, first_new, second_new, weight_full - rate * change)


def ring_place(index, slot):
    offset = jnp.where(slot == 0, 0, jnp.where(slot == 1, 3, jnp.where(slot == 2, 1, 2)))
    return (index + offset) % 4


def attention(queries, keyval, visible, scale):
    head = queries.shape[-1]
    scores = dot("sqh,skh->sqk", queries, keyval[..., :head]) * scale
    scores = jnp.where(visible, scores, MASKED)
    top = jnp.max(scores, axis=-1, keepdims=True)
    lse = top + jnp.log(jnp.sum(jnp.exp(scores - top), axis=-1, keepdims=True))
    probs = jnp.exp(scores - lse)
    return dot("sqk,skh->sqh", probs.astype(BF), keyval[..., head:]).astype(BF), lse


def attention_back(queries, keyval, visible, scale, lse, upstream):
    head = queries.shape[-1]
    scores = dot("sqh,skh->sqk", queries, keyval[..., :head]) * scale
    probs = jnp.exp(jnp.where(visible, scores, MASKED) - lse)
    d_probs = dot("sqh,skh->sqk", upstream, keyval[..., head:])
    inner = jnp.sum(d_probs * probs, axis=-1, keepdims=True)
    d_scores = (probs * (d_probs - inner)).astype(BF)
    d_queries = dot("sqk,skh->sqh", d_scores, keyval[..., :head]) * scale
    d_keys = dot("sqk,sqh->skh", d_scores, queries) * scale
    d_values = dot("sqk,sqh->skh", probs.astype(BF), upstream)
    return d_queries, jnp.concatenate([d_keys, d_values], axis=-1).astype(BF)


def shards(
    block_input,
    positions,
    cotangent,
    query_weight,
    keyval_weight,
    output_weight,
    gateup_weight,
    down_weight,
    norm_gains,
    query_first,
    query_second,
    keyval_first,
    keyval_second,
    output_first,
    output_second,
    gateup_first,
    gateup_second,
    down_first,
    down_second,
    gains_first,
    gains_second,
):
    seqs, rows, width = block_input.shape
    head = keyval_weight.shape[1] // 2
    quarter = rows // 4
    own = seqs * quarter
    tokens = 4 * own
    scale = head ** (-0.5)
    x_at, zh_at, y_at, zl_at, core_at = (
        lax.axis_index(axis) for axis in ("x", "zh", "y", "zl", "core")
    )
    member = zl_at * 2 + core_at
    context_at = zh_at * 4 + y_at
    row_piece = query_weight.shape[0]

    part = keyval_weight.shape[0]
    gain_piece = norm_gains.shape[0]
    pad = 2 * head - gain_piece
    piece = jnp.concatenate([keyval_weight, jnp.pad(norm_gains, (0, pad)).reshape(1, -1)])
    piece = by_bit(core_at, piece, flip(piece, "core"))
    piece = by_bit(zl_at, piece, flip(piece, "zl"))
    narrow = jnp.concatenate([query_weight, output_weight.T], axis=1)
    piece = jnp.concatenate([piece.reshape(4 * (part + 1), 2 * head), narrow])
    piece, gateup_ready, down_ready = lax.optimization_barrier(
        (by_bit(zh_at, piece, flip(piece, "zh")), gateup_weight, down_weight)
    )
    narrow_rows = piece[:, 4 * (part + 1) :].reshape(2 * row_piece, 2 * head)
    piece = piece[:, : 4 * (part + 1)].reshape(8, part + 1, 2 * head)
    keyval_rows = piece[:, :part].reshape(8 * part, 2 * head)
    small = lax.optimization_barrier(jnp.concatenate([narrow_rows, piece[:, part]]))
    keyval_rows = lax.optimization_barrier(keyval_rows)
    line = jnp.concatenate(ring_gather(small, "x"))
    keyval_line = jnp.concatenate(ring_gather(keyval_rows, "y"))
    line, keyval_line, block_input, positions, x_at = lax.optimization_barrier(
        (line, keyval_line, block_input, positions, x_at)
    )
    small = jnp.concatenate(ring_gather(line, "y")).reshape(16, -1, 2 * head)
    full_keyval = jnp.stack(ring_gather(keyval_line, "x")).reshape(4, 4, 2 * row_piece, -1)
    full_keyval = full_keyval.transpose(1, 0, 2, 3).reshape(width, 2 * head)
    units = down_weight.shape[0]
    half_units = units // 2
    lanes = -(-half_units // 128) * 128
    fill = ((0, 0), (0, lanes - half_units))
    wide_parts = (gateup_ready[:, 0], gateup_ready[:, 1], down_ready.T)
    lower = jnp.concatenate([jnp.pad(w[:, :half_units], fill) for w in wide_parts], axis=1)
    upper = jnp.concatenate([jnp.pad(w[:, half_units:], fill) for w in wide_parts], axis=1)
    keep = jnp.where(zh_at == 0, lower, upper)
    send = jnp.where(zh_at == 0, upper, lower)
    bundle = by_bit(zh_at, keep, flip(send, "zh")).reshape(2 * row_piece, -1)
    bundle, small, full_keyval = lax.optimization_barrier((bundle, small, full_keyval))
    big = lax.all_gather(bundle, ("x", "y"), axis=0, tiled=True)
    full_query = small[:, : 2 * row_piece, :head].reshape(width, head)
    full_output = small[:, : 2 * row_piece, head:].reshape(width, head)
    place = lax.broadcasted_iota(jnp.int32, (width, width), 1)
    source_row = lax.broadcasted_iota(jnp.int32, (width, width), 0)
    group = place // (2 * row_piece)
    inner_row = ((place // row_piece) % 2) * 4 * row_piece + place % row_piece
    straight = (source_row == inner_row + ((group // 4) * 8 + group % 4) * row_piece).astype(BF)
    round_x, round_y = ring_place(x_at, group % 4), ring_place(y_at, group // 4)
    round_block, source_block = round_x * 8 + round_y, round_x * 4 + round_y
    round_order = (source_row == inner_row + round_block * row_piece).astype(BF)
    to_round = (source_row == source_block * 2 * row_piece + place % (2 * row_piece)).astype(BF)

    slot = lax.broadcasted_iota(jnp.int32, (128, 128), 1)
    holder = (
        (ring_place(x_at, (slot // 8) % 4) * 2 + (slot // 4) % 2) * 4
        + ring_place(y_at, slot // 32)
    ) * 4 + slot % 4
    holder = (lax.broadcasted_iota(jnp.int32, (128, 128), 0) == holder).astype(BF)
    gain_rows = small[:, 2 * row_piece :, :128].reshape(128, 128)
    gains_all = dot("ar,rg->ag", holder, gain_rows)[:, :gain_piece].astype(BF).reshape(-1)
    model_gains = gains_all[: 4 * width].reshape(4, width)
    attn_in_gain = lax.optimization_barrier(dot("gd,de->ge", model_gains, round_order))[0]
    straight_gains = dot("gd,de->ge", model_gains, straight)
    attn_out_gain, ffn_in_gain, ffn_out_gain = (straight_gains[i] for i in range(1, 4))
    query_gain = gains_all[4 * width : 4 * width + head].astype(F32)
    key_gain = gains_all[4 * width + head :].astype(F32)

    starts = [(member ^ k) * quarter for k in range(4)]

    def quarters(array):
        return jnp.concatenate(
            [lax.dynamic_slice_in_dim(array, start, quarter, 1) for start in starts], axis=1
        )

    def own_of(array):
        return array.reshape(seqs, 4, quarter, -1)[:, 0].reshape(own, -1)

    token_rows = quarters(block_input).reshape(tokens, width)
    inputs = dot("td,de->te", token_rows, round_order)
    own_inputs = dot("td,de->te", own_of(token_rows), straight)
    own_cotangent = lax.dynamic_slice_in_dim(cotangent, starts[0], quarter, 1)
    upstream = dot("td,de->te", own_cotangent.reshape(own, width), straight)
    place_of = quarters(positions)
    cosine, sine = rotation(place_of.reshape(tokens), head)

    normed = rms_norm(inputs, attn_in_gain).astype(BF)
    query_raw = dot("td,dh->th", normed, full_query)
    raw = dot("td,dh->th", normed, full_keyval)
    key_raw, value_raw = raw[:, :head], raw[:, head:]
    queries = rotate(rms_norm(query_raw, query_gain), cosine, sine).astype(BF)
    key_rows = rotate(rms_norm(key_raw, key_gain), cosine, sine)
    keyval = jnp.concatenate([key_rows, value_raw], axis=1).astype(BF)
    keyval = keyval.reshape(seqs, 4, quarter, 2 * head)
    half = keyval[:, 0::2]
    got = jnp.stack(
        [
            lax.ppermute(half, ("zh", "y"), [(i, i + back) for i in range(8 - back)])
            for back in range(BACK, 0, -1)
        ],
        axis=1,
    )
    other = flip(got, "core")
    keys_all = jnp.concatenate(
        [array.reshape(seqs, -1, 2 * head) for array in (got, other, keyval)], axis=1
    )
    reach = BACK * rows // 2

    def position_of(block, place_in, row):
        return (context_at + block) * rows + (member ^ place_in) * quarter + row

    index = lax.broadcasted_iota(jnp.int32, (1, rows, 1), 1)
    query_index = position_of(0, index // quarter, index % quarter)
    index = lax.broadcasted_iota(jnp.int32, (1, 1, 2 * reach + rows), 2)
    before = index < 2 * reach
    block = jnp.where(before, (index % reach) // (rows // 2) - BACK, 0)
    slot = jnp.where(
        before, (index // quarter) % 2 * 2 + index // reach, (index - 2 * reach) // quarter
    )
    key_index = position_of(block, slot, index % quarter)
    first_key = query_index - place_of[:, :, None]
    visible = (key_index <= query_index) & (key_index >= first_key)

    sequence_queries = queries.reshape(seqs, rows, head)
    attended, lse = attention(sequence_queries, keys_all, visible, scale)
    attended = attended.reshape(tokens, head)
    projected = token_scatter(
        dot("th,dh->td", attended, full_output).reshape(seqs, 4, quarter, width)
    ).reshape(own, width)
    high = projected.astype(BF)
    both = jnp.concatenate([high, (projected - high.astype(F32)).astype(BF)])
    both = dot("te,de->td", both, to_round)
    projected = both[:own] + both[own:]
    middle = own_inputs + rms_norm(projected, attn_out_gain)
    ffn_own = rms_norm(middle, ffn_in_gain).astype(BF)
    four = ring_gather(ffn_own, DEPTH)
    four[1], big = lax.optimization_barrier((four[1], big))
    full_gateup, full_down = big[:, : 2 * lanes], big[:, 2 * lanes :]
    four = jnp.stack(four)
    ffn_in = jnp.concatenate([four, flip(four, "core")]).reshape(2 * tokens, width)
    gate_up = dot("td,df->tf", ffn_in, full_gateup)

    def geglu(pair):
        return jax.nn.gelu(pair[:, :lanes], approximate=True) * pair[:, lanes:]

    hidden = geglu(gate_up).astype(BF)
    down_sum = wide_scatter(dot("tf,df->td", hidden, full_down).reshape(8, own, width))
    own_output = (middle + rms_norm(down_sum, ffn_out_gain)).astype(BF)

    def to_whole(plain):
        parts = token_gather(plain.reshape(seqs, quarter, width))
        whole = jnp.zeros((seqs, rows, width), BF)
        for k in range(4):
            whole = lax.dynamic_update_slice_in_dim(whole, parts[:, k], starts[k], 1)
        return whole

    d_down, grad_ffn_out = rms_back(down_sum, ffn_out_gain, upstream)
    d_down = wide_gather(d_down.astype(BF)).reshape(2 * tokens, width)
    d_hidden = dot("td,df->tf", d_down, full_down)
    gate_up, d_hidden = lax.optimization_barrier((gate_up, d_hidden))
    unused_hidden, geglu_back = jax.vjp(geglu, gate_up)
    d_gateup = geglu_back(d_hidden)[0].astype(BF)
    parts = dot("tf,df->td", d_gateup, full_gateup).reshape(8, own, width)
    parts = parts[:4].astype(F32) + flip(parts[4:].astype(BF), "core").astype(F32)
    low = parts.astype(BF)
    ffn_term = jnp.concatenate(
        [dot("td,tf->df", ffn_in, d_gateup).astype(BF), dot("td,tf->df", d_down, hidden).astype(BF)],
        axis=1,
    )
    got = [shift(low[1], DEPTH, -1), shift(low[2], DEPTH, 1), shift(low[3], DEPTH, 2)]
    got, ffn_term = lax.optimization_barrier((got, ffn_term))
    d_ffn = parts[0] + got[0].astype(F32) + got[1].astype(F32) + got[2].astype(F32)
    ffn_rows = lax.psum_scatter(ffn_term, ("x", "y"), scatter_dimension=0, tiled=True)
    d_middle, grad_ffn_in = rms_back(middle, ffn_in_gain, d_ffn)
    d_middle = upstream + d_middle
    d_projected, grad_attn_out = rms_back(projected, attn_out_gain, d_middle)
    d_projected = dot("te,ed->td", d_projected.astype(BF), to_round).astype(BF)
    d_projected = token_gather(d_projected.reshape(seqs, quarter, width)).reshape(tokens, width)
    d_attended = dot("td,dh->th", d_projected, full_output).astype(BF)
    d_queries, d_keyval = attention_back(
        sequence_queries,
        keys_all,
        visible,
        scale,
        lse,
        d_attended.reshape(seqs, rows, head),
    )
    d_queries = d_queries.reshape(tokens, head)
    d_own = d_keyval[:, 2 * reach :].reshape(seqs, 1, 4, quarter, 2 * head)
    grid = (seqs, BACK, 2, quarter, 2 * head)
    d_got, d_other = d_keyval[:, :reach].reshape(grid), d_keyval[:, reach : 2 * reach].reshape(grid)
    got = flip(jnp.concatenate([d_other, d_own[:, :, 1::2]], axis=1), "core")
    halves = jnp.concatenate([d_got, d_own[:, :, 0::2]], axis=1).astype(F32) + got.astype(F32)
    terms = [
        lax.ppermute(
            halves[:, BACK - back].astype(BF),
            ("zh", "y"),
            [(i + back, i) for i in range(8 - back)],
        )
        for back in range(1, BACK + 1)
    ]
    terms[0], d_queries = lax.optimization_barrier((terms[0], d_queries))

    def query_path(raw_rows, gain):
        return rotate(rms_norm(raw_rows, gain), cosine, sine)

    def key_path(raw_rows, gain):
        return rotate(rms_norm(raw_rows, gain), own_of(cosine), own_of(sine))

    unused_query, query_back = jax.vjp(query_path, query_raw, query_gain)
    d_query_raw, grad_query = query_back(d_queries)
    d_query_raw = d_query_raw.astype(BF)
    query_term = dot("td,th->dh", normed, d_query_raw).astype(BF)
    half = halves[:, BACK]
    for term in terms:
        half = half + term.astype(F32)
    d_keyval = half[:, 0] + flip(half[:, 1].astype(BF), "zl").astype(F32)
    d_keyval = d_keyval.reshape(own, 2 * head)
    d_keyval, d_projected, d_middle, query_term = lax.optimization_barrier(
        (d_keyval, d_projected, d_middle, query_term)
    )
    output_term = dot("td,th->dh", d_projected, attended).astype(BF)
    narrow_term = jnp.concatenate([query_term, output_term], axis=1).reshape(16, -1, 2 * head)
    narrow_line = ring_scatter([narrow_term[4 * i : 4 * i + 4] for i in range(4)], "y").astype(BF)
    narrow_rows = ring_scatter([narrow_line[i] for i in range(4)], "x")
    d_normed_query = dot("th,dh->td", d_query_raw, full_query)
    d_normed = token_scatter(d_normed_query.reshape(seqs, 4, quarter, width)).reshape(own, width)
    unused_key, key_back = jax.vjp(key_path, own_of(key_raw), key_gain)
    d_key_raw, grad_key = key_back(d_keyval[:, :head])
    d_keyval_raw = jnp.concatenate([d_key_raw, d_keyval[:, head:]], axis=1).astype(BF)
    columns = 2 * head // 4
    column_parts = exchange(
        [
            lax.dynamic_slice_in_dim(d_keyval_raw, (member ^ k) * columns, columns, 1)
            for k in range(4)
        ]
    )
    column_rows = jnp.stack([v.reshape(seqs, quarter, columns) for v in column_parts], axis=1)
    keyval_term = dot("td,tk->dk", normed, column_rows.reshape(tokens, columns)).astype(BF)
    d_normed_keyval = dot("tk,dk->td", d_keyval_raw, full_keyval)
    inverse = inverse_rms(inputs)
    round_inputs = own_of(inputs)
    grad_attn_in = jnp.sum(d_normed_query * inputs * inverse, axis=0) + jnp.sum(
        d_normed_keyval * round_inputs * own_of(inverse), axis=0
    )
    wide = jnp.stack([grad_attn_out, grad_ffn_in, grad_ffn_out]).astype(BF)
    total = jnp.concatenate(
        [
            dot("ge,de->gd", grad_attn_in.astype(BF).reshape(1, -1), round_order).reshape(-1),
            dot("ge,de->gd", wide, straight).reshape(-1),
            grad_query,
            grad_key,
        ]
    )
    total = total.astype(BF).reshape(128, gain_piece)
    total = dot("ar,ag->rg", holder, jnp.pad(total, ((0, 0), (0, columns - gain_piece))))
    terms = jnp.concatenate(
        [keyval_term.reshape(16, -1, columns), total.astype(BF).reshape(16, 8, columns)], axis=1
    )
    terms, ffn_rows, narrow_rows = lax.optimization_barrier((terms, ffn_rows, narrow_rows))
    got = [
        shift(terms[4:8], "y", -1), shift(terms[8:12], "y", 1), shift(terms[12:], "y", 2)
    ]
    got[0], own_output, d_normed = lax.optimization_barrier((got[0], own_output, d_normed))
    terms = sum((value.astype(F32) for value in got), terms[:4].astype(F32)).astype(BF)
    terms = ring_scatter([terms[i] for i in range(4)], "x")
    d_inputs, unused_gain = rms_back(round_inputs, attn_in_gain, d_normed + d_normed_keyval)
    input_grad = dot("te,de->td", d_middle.astype(BF), straight) + dot(
        "te,de->td", d_inputs.astype(BF), round_order
    )
    input_grad = to_whole(input_grad.astype(BF)).astype(F32)
    block_output = to_whole(dot("te,de->td", own_output, straight).astype(BF))
    narrow_low = narrow_rows.astype(BF)
    theirs = jnp.concatenate(
        [
            jnp.where(zh_at == 0, ffn_rows[row_piece:], ffn_rows[:row_piece]),
            jnp.where(zh_at == 0, narrow_low[row_piece:], narrow_low[:row_piece]),
        ],
        axis=1,
    )
    over = flip(theirs, "zh")
    mine = jnp.where(zh_at == 0, ffn_rows[:row_piece], ffn_rows[row_piece:])
    both = by_bit(zh_at, mine, over[:, : 3 * lanes]).astype(F32)
    gate_grad, up_grad, down_grad = (
        jnp.concatenate(
            [both[i][:, lanes * j : lanes * j + half_units] for i in range(2)], axis=1
        )
        for j in range(3)
    )
    gateup_grad = jnp.stack([gate_grad, up_grad], axis=1)
    down_grad = down_grad.T
    mine = jnp.where(zh_at == 0, narrow_rows[:row_piece], narrow_rows[row_piece:])
    narrow_grad = mine + over[:, 3 * lanes :].astype(F32)
    query_grad = narrow_grad[:, :head]
    output_grad = narrow_grad[:, head:].T
    query_results = adam_step(query_weight, query_grad, query_first, query_second, True)
    output_results = adam_step(output_weight, output_grad, output_first, output_second, True)
    gateup_results = adam_step(gateup_weight, gateup_grad, gateup_first, gateup_second, True)
    down_results = adam_step(down_weight, down_grad, down_first, down_second, True)
    terms, query_results, output_results, gateup_results, down_results = lax.optimization_barrier(
        (terms, query_results, output_results, gateup_results, down_results)
    )
    keyval_part = terms[: 2 * row_piece].reshape(2, 4, part, columns)
    gain_part = terms[2 * row_piece :].reshape(2, 4, 1, columns)
    both = jnp.concatenate([keyval_part, gain_part], axis=2)
    mine = jnp.where(zh_at == 0, both[0], both[1])
    theirs = jnp.where(zh_at == 0, both[1], both[0]).astype(BF)
    mine = mine + flip(theirs, "zh").astype(F32)
    owners = exchange(
        [lax.dynamic_index_in_dim(mine, member ^ k, 0, keepdims=False) for k in range(4)]
    )
    keyval_grad = jnp.zeros((part, 2 * head), F32)
    gains_grad = jnp.zeros((gain_piece,), F32)
    for k in range(4):
        keyval_grad = lax.dynamic_update_slice_in_dim(
            keyval_grad, owners[k][:part], (member ^ k) * columns, 1
        )
        gains_grad = gains_grad + owners[k][part, :gain_piece]

    results = [block_output, input_grad]
    results.extend(query_results)
    results.extend(adam_step(keyval_weight, keyval_grad, keyval_first, keyval_second, True))
    results.extend(output_results)
    results.extend(gateup_results)
    results.extend(down_results)
    results.extend(adam_step(norm_gains, gains_grad, gains_first, gains_second, False))
    return tuple(results)


def solution(mesh):
    fine = Mesh(mesh.devices.reshape(4, 2, 4, 2, 2), ("x", "zh", "y", "zl", "core"))
    context = ("zh", "y")
    tensor = ("zl", "core")
    fsdp = ("x", "zh", "y")
    everything = fsdp + tensor
    stream = P("x", context, None)
    query = P(fsdp, tensor)
    keyval = P(everything, None)
    output = P(tensor, fsdp)
    gateup = P(fsdp, None, tensor)
    gains = P(everything)
    return jax.shard_map(
        shards,
        mesh=fine,
        in_specs=(
            stream, P("x", context), stream,
            query, keyval, output, gateup, output, gains,
            query, query, keyval, keyval, output, output,
            gateup, gateup, output, output, gains, gains,
        ),
        out_specs=(stream, stream)
        + (query,) * 4
        + (keyval,) * 4
        + (output,) * 4
        + (gateup,) * 4
        + (output,) * 4
        + (gains,) * 4,
        check_vma=False,
    )
```

```python
import jax
import jax.numpy as jnp
from jax import lax
from jax.experimental import pallas as pl
from jax.experimental.pallas import tpu as pltpu
from jax.sharding import Mesh
from jax.sharding import PartitionSpec as P

STEP = 4
EPSILON = 1e-06
ROPE_BASE = 1000000.0
LEARN_RATE = 0.02
GAIN_RATE = 0.5
WEIGHT_DECAY = 0.1
BETA_ONE = 0.5
BETA_TWO = 0.5
ADAM_EPS = 1e-08
MASKED = -1e30
BACK = 4

BF = jnp.bfloat16
F32 = jnp.float32


def dot(spec, left, right):
    return jnp.einsum(spec, left, right, preferred_element_type=F32)


def shift(value, axis, step):
    size = 4 if isinstance(axis, tuple) else lax.axis_size(axis)
    return lax.ppermute(value, axis, [(i, (i + step) % size) for i in range(size)])


def flip(value, axis):
    return shift(value, axis, 1)


def ring_gather(value, axis):
    return [value, shift(value, axis, 1), shift(value, axis, -1), shift(value, axis, 2)]


def ring_scatter(parts, axis):
    got = [shift(parts[1], axis, -1), shift(parts[2], axis, 1), shift(parts[3], axis, 2)]
    return parts[0].astype(F32) + got[0].astype(F32) + got[1].astype(F32) + got[2].astype(F32)


def by_bit(bit, mine, theirs):
    first = jnp.where(bit == 0, mine, theirs)
    return jnp.stack([first, jnp.where(bit == 0, theirs, mine)])


DEPTH = ("zh", "zl")


def wide_gather(own):
    four = jnp.stack(ring_gather(own, DEPTH))
    return jnp.concatenate([four, flip(four, "core")])


def wide_scatter(parts):
    got = flip(parts[4:].astype(BF), "core")
    four = parts[:4].astype(F32) + got.astype(F32)
    low = four.astype(BF)
    return ring_scatter([four[0], low[1], low[2], low[3]], DEPTH)


def token_gather(own):
    two = jnp.stack([own, flip(own, "zl")], axis=1)
    other = flip(two, "core")
    return jnp.stack([two[:, 0], other[:, 0], two[:, 1], other[:, 1]], axis=1)


def token_scatter(parts):
    got = flip(parts[:, 1::2].astype(BF), "core").astype(F32)
    mine = parts[:, 0].astype(F32) + got[:, 0]
    theirs = (parts[:, 2].astype(F32) + got[:, 1]).astype(BF)
    return mine + flip(theirs, "zl").astype(F32)


def exchange(parts):
    got = flip(jnp.stack([parts[1], parts[3]]), "core")
    over = flip(jnp.stack([parts[2], got[1]]), "zl")
    return [parts[0], got[0], over[0], over[1]]


def inverse_rms(vector):
    return lax.rsqrt(jnp.mean(vector * vector, axis=-1, keepdims=True) + EPSILON)


def rms_norm(vector, gain):
    return vector * inverse_rms(vector) * gain


def rms_back(vector, gain, upstream):
    inverse = inverse_rms(vector)
    scaled = upstream * gain
    inner = jnp.mean(scaled * vector, axis=-1, keepdims=True)
    return (
        inverse * (scaled - vector * (inverse * inverse) * inner),
        jnp.sum(upstream * vector * inverse, axis=0),
    )


def rotation(positions, head_size):
    half_size = head_size // 2
    inverse = jnp.exp(
        jnp.arange(half_size, dtype=F32) * (-2.0 * jnp.log(ROPE_BASE) / head_size)
    )
    angles = positions.astype(F32)[..., None] * inverse
    return jnp.cos(angles), jnp.sin(angles)


def rotate(vector, cosine, sine):
    half_size = vector.shape[-1] // 2
    first_half = vector[..., :half_size]
    second_half = vector[..., half_size:]
    return jnp.concatenate(
        [first_half * cosine - second_half * sine, second_half * cosine + first_half * sine],
        axis=-1,
    )


def adam_step(weight, gradient, first_old, second_old, decayed):
    weight_full = weight.astype(F32)
    first_new = BETA_ONE * first_old + (1.0 - BETA_ONE) * gradient
    second_new = BETA_TWO * second_old + (1.0 - BETA_TWO) * gradient * gradient
    first_hat = first_new / (1.0 - BETA_ONE**STEP)
    second_hat = second_new / (1.0 - BETA_TWO**STEP)
    change = first_hat / (jnp.sqrt(second_hat) + ADAM_EPS)
    if decayed:
        change = change + WEIGHT_DECAY * weight_full
        rate = LEARN_RATE
    else:
        rate = GAIN_RATE
    return (gradient, first_new, second_new, weight_full - rate * change)


def ring_place(index, slot):
    offset = jnp.where(slot == 0, 0, jnp.where(slot == 1, 3, jnp.where(slot == 2, 1, 2)))
    return (index + offset) % 4


def attention(queries, keyval, visible, scale):
    head = queries.shape[-1]
    scores = dot("sqh,skh->sqk", queries, keyval[..., :head]) * scale
    scores = jnp.where(visible, scores, MASKED)
    top = jnp.max(scores, axis=-1, keepdims=True)
    lse = top + jnp.log(jnp.sum(jnp.exp(scores - top), axis=-1, keepdims=True))
    probs = jnp.exp(scores - lse)
    return dot("sqk,skh->sqh", probs.astype(BF), keyval[..., head:]).astype(BF), lse


def tile_dot(left, right, left_dim, right_dim):
    return lax.dot_general(
        left, right, (((left_dim,), (right_dim,)), ((), ())), preferred_element_type=F32
    )


def attention_back_kernel(
    scale, queries, keyval, at, first, key_at, lse, upstream, d_queries, d_keyval
):
    head = queries.shape[-1]
    keys, values = keyval[0, :, :head], keyval[0, :, head:]
    rows, grads = queries[0], upstream[0]
    place = key_at[...]
    visible = (place <= at[...]) & (place >= first[0])
    scores = tile_dot(rows, keys, 1, 1) * scale
    probs = jnp.exp(jnp.where(visible, scores, MASKED) - lse[0])
    d_probs = tile_dot(grads, values, 1, 1)
    inner = jnp.sum(d_probs * probs, axis=-1, keepdims=True)
    d_scores = (probs * (d_probs - inner)).astype(BF)
    d_queries[0] = tile_dot(d_scores, keys, 1, 0) * scale
    d_keyval[0, :, :head] = (tile_dot(d_scores, rows, 0, 0) * scale).astype(BF)
    d_keyval[0, :, head:] = tile_dot(probs.astype(BF), grads, 0, 0).astype(BF)


def attention_back(queries, keyval, at, first, key_at, scale, lse, upstream):
    seqs, rows, head = queries.shape
    keys = keyval.shape[1]

    def kernel(*refs):
        attention_back_kernel(scale, *refs)

    def block(*shape):
        return pl.BlockSpec((1,) + shape, lambda i: (i, 0, 0))

    return pl.pallas_call(
        kernel,
        grid=(seqs,),
        in_specs=[
            block(rows, head),
            block(keys, 2 * head),
            pl.BlockSpec((rows, 1), lambda i: (0, 0)),
            block(rows, 1),
            pl.BlockSpec((1, keys), lambda i: (0, 0)),
            block(rows, 1),
            block(rows, head),
        ],
        out_specs=[block(rows, head), block(keys, 2 * head)],
        out_shape=[
            jax.ShapeDtypeStruct((seqs, rows, head), F32),
            jax.ShapeDtypeStruct((seqs, keys, 2 * head), BF),
        ],
        compiler_params=pltpu.CompilerParams(vmem_limit_bytes=40 * 1024 * 1024),
        cost_estimate=pl.CostEstimate(
            flops=10 * seqs * rows * keys * head,
            bytes_accessed=8 * seqs * keys * head,
            transcendentals=seqs * rows * keys,
        ),
    )(queries, keyval, at, first, key_at, lse, upstream)


def shards(
    block_input,
    positions,
    cotangent,
    query_weight,
    keyval_weight,
    output_weight,
    gateup_weight,
    down_weight,
    norm_gains,
    query_first,
    query_second,
    keyval_first,
    keyval_second,
    output_first,
    output_second,
    gateup_first,
    gateup_second,
    down_first,
    down_second,
    gains_first,
    gains_second,
):
    seqs, rows, width = block_input.shape
    head = keyval_weight.shape[1] // 2
    quarter = rows // 4
    own = seqs * quarter
    tokens = 4 * own
    scale = head ** (-0.5)
    x_at, zh_at, y_at, zl_at, core_at = (
        lax.axis_index(axis) for axis in ("x", "zh", "y", "zl", "core")
    )
    member = zl_at * 2 + core_at
    context_at = zh_at * 4 + y_at
    row_piece = query_weight.shape[0]

    part = keyval_weight.shape[0]
    gain_piece = norm_gains.shape[0]
    pad = 2 * head - gain_piece
    piece = jnp.concatenate([keyval_weight, jnp.pad(norm_gains, (0, pad)).reshape(1, -1)])
    piece = by_bit(core_at, piece, flip(piece, "core"))
    piece = by_bit(zl_at, piece, flip(piece, "zl"))
    narrow = jnp.concatenate([query_weight, output_weight.T], axis=1)
    piece = jnp.concatenate([piece.reshape(4 * (part + 1), 2 * head), narrow])
    piece, gateup_ready, down_ready = lax.optimization_barrier(
        (by_bit(zh_at, piece, flip(piece, "zh")), gateup_weight, down_weight)
    )
    narrow_rows = piece[:, 4 * (part + 1) :].reshape(2 * row_piece, 2 * head)
    piece = piece[:, : 4 * (part + 1)].reshape(8, part + 1, 2 * head)
    keyval_rows = piece[:, :part].reshape(8 * part, 2 * head)
    small = lax.optimization_barrier(jnp.concatenate([narrow_rows, piece[:, part]]))
    keyval_rows = lax.optimization_barrier(keyval_rows)
    line = jnp.concatenate(ring_gather(small, "x"))
    keyval_line = jnp.concatenate(ring_gather(keyval_rows, "y"))
    line, keyval_line = lax.optimization_barrier((line, keyval_line))
    small = jnp.concatenate(ring_gather(line, "y")).reshape(16, -1, 2 * head)
    lines = ring_gather(keyval_line, "x")
    lines[1], block_input, positions, x_at = lax.optimization_barrier(
        (lines[1], block_input, positions, x_at)
    )
    full_keyval = jnp.stack(lines).reshape(4, 4, 2 * row_piece, -1)
    full_keyval = full_keyval.transpose(1, 0, 2, 3).reshape(width, 2 * head)
    units = down_weight.shape[0]
    half_units = units // 2
    lanes = -(-half_units // 128) * 128
    fill = ((0, 0), (0, lanes - half_units))
    wide_parts = (gateup_ready[:, 0], gateup_ready[:, 1], down_ready.T)
    lower = jnp.concatenate([jnp.pad(w[:, :half_units], fill) for w in wide_parts], axis=1)
    upper = jnp.concatenate([jnp.pad(w[:, half_units:], fill) for w in wide_parts], axis=1)
    keep = jnp.where(zh_at == 0, lower, upper)
    send = jnp.where(zh_at == 0, upper, lower)
    bundle = by_bit(zh_at, keep, flip(send, "zh")).reshape(2 * row_piece, -1)
    bundle, small, full_keyval = lax.optimization_barrier((bundle, small, full_keyval))
    big = lax.all_gather(bundle, ("x", "y"), axis=0, tiled=True)
    full_query = small[:, : 2 * row_piece, :head].reshape(width, head)
    full_output = small[:, : 2 * row_piece, head:].reshape(width, head)
    place = lax.broadcasted_iota(jnp.int32, (width, width), 1)
    source_row = lax.broadcasted_iota(jnp.int32, (width, width), 0)
    group = place // (2 * row_piece)
    inner_row = ((place // row_piece) % 2) * 4 * row_piece + place % row_piece
    straight = (source_row == inner_row + ((group // 4) * 8 + group % 4) * row_piece).astype(BF)
    round_x, round_y = ring_place(x_at, group % 4), ring_place(y_at, group // 4)
    round_block, source_block = round_x * 8 + round_y, round_x * 4 + round_y
    round_order = (source_row == inner_row + round_block * row_piece).astype(BF)
    to_round = (source_row == source_block * 2 * row_piece + place % (2 * row_piece)).astype(BF)

    slot = lax.broadcasted_iota(jnp.int32, (128, 128), 1)
    holder = (
        (ring_place(x_at, (slot // 8) % 4) * 2 + (slot // 4) % 2) * 4
        + ring_place(y_at, slot // 32)
    ) * 4 + slot % 4
    holder = (lax.broadcasted_iota(jnp.int32, (128, 128), 0) == holder).astype(BF)
    gain_rows = small[:, 2 * row_piece :, :128].reshape(128, 128)
    gains_all = dot("ar,rg->ag", holder, gain_rows)[:, :gain_piece].astype(BF).reshape(-1)
    model_gains = gains_all[: 4 * width].reshape(4, width)
    attn_in_gain = lax.optimization_barrier(dot("gd,de->ge", model_gains, round_order))[0]
    straight_gains = dot("gd,de->ge", model_gains, straight)
    attn_out_gain, ffn_in_gain, ffn_out_gain = (straight_gains[i] for i in range(1, 4))
    query_gain = gains_all[4 * width : 4 * width + head].astype(F32)
    key_gain = gains_all[4 * width + head :].astype(F32)

    starts = [(member ^ k) * quarter for k in range(4)]

    def quarters(array):
        return jnp.concatenate(
            [lax.dynamic_slice_in_dim(array, start, quarter, 1) for start in starts], axis=1
        )

    def own_of(array):
        return array.reshape(seqs, 4, quarter, -1)[:, 0].reshape(own, -1)

    token_rows = quarters(block_input).reshape(tokens, width)
    inputs = dot("td,de->te", token_rows, round_order)
    own_inputs = dot("td,de->te", own_of(token_rows), straight)
    own_cotangent = lax.dynamic_slice_in_dim(cotangent, starts[0], quarter, 1)
    upstream = dot("td,de->te", own_cotangent.reshape(own, width), straight)
    place_of = quarters(positions)
    cosine, sine = rotation(place_of.reshape(tokens), head)

    normed = rms_norm(inputs, attn_in_gain).astype(BF)
    query_raw = dot("td,dh->th", normed, full_query)
    raw = dot("td,dh->th", normed, full_keyval)
    key_raw, value_raw = raw[:, :head], raw[:, head:]
    queries = rotate(rms_norm(query_raw, query_gain), cosine, sine).astype(BF)
    key_rows = rotate(rms_norm(key_raw, key_gain), cosine, sine)
    keyval = jnp.concatenate([key_rows, value_raw], axis=1).astype(BF)
    keyval = keyval.reshape(seqs, 4, quarter, 2 * head)
    half = keyval[:, 0::2]
    got = jnp.stack(
        [
            lax.ppermute(half, ("zh", "y"), [(i, i + back) for i in range(8 - back)])
            for back in range(BACK, 0, -1)
        ],
        axis=1,
    )
    other = flip(got, "core")
    keys_all = jnp.concatenate(
        [array.reshape(seqs, -1, 2 * head) for array in (got, other, keyval)], axis=1
    )
    reach = BACK * rows // 2

    def position_of(block, place_in, row):
        return (context_at + block) * rows + (member ^ place_in) * quarter + row

    index = lax.broadcasted_iota(jnp.int32, (1, rows, 1), 1)
    query_index = position_of(0, index // quarter, index % quarter)
    index = lax.broadcasted_iota(jnp.int32, (1, 1, 2 * reach + rows), 2)
    before = index < 2 * reach
    block = jnp.where(before, (index % reach) // (rows // 2) - BACK, 0)
    slot = jnp.where(
        before, (index // quarter) % 2 * 2 + index // reach, (index - 2 * reach) // quarter
    )
    key_index = position_of(block, slot, index % quarter)
    first_key = query_index - place_of[:, :, None]
    visible = (key_index <= query_index) & (key_index >= first_key)

    sequence_queries = queries.reshape(seqs, rows, head)
    attended, lse = attention(sequence_queries, keys_all, visible, scale)
    attended = attended.reshape(tokens, head)
    projected = token_scatter(
        dot("th,dh->td", attended, full_output).reshape(seqs, 4, quarter, width)
    ).reshape(own, width)
    high = projected.astype(BF)
    both = jnp.concatenate([high, (projected - high.astype(F32)).astype(BF)])
    both = dot("te,de->td", both, to_round)
    projected = both[:own] + both[own:]
    middle = own_inputs + rms_norm(projected, attn_out_gain)
    ffn_own = rms_norm(middle, ffn_in_gain).astype(BF)
    four = ring_gather(ffn_own, DEPTH)
    four[1], big = lax.optimization_barrier((four[1], big))
    full_gateup, full_down = big[:, : 2 * lanes], big[:, 2 * lanes :]
    four = jnp.stack(four)
    ffn_in = jnp.concatenate([four, flip(four, "core")]).reshape(2 * tokens, width)
    gate_up = dot("td,df->tf", ffn_in, full_gateup)

    def geglu(pair):
        return jax.nn.gelu(pair[:, :lanes], approximate=True) * pair[:, lanes:]

    hidden = geglu(gate_up).astype(BF)
    down_sum = wide_scatter(dot("tf,df->td", hidden, full_down).reshape(8, own, width))
    own_output = (middle + rms_norm(down_sum, ffn_out_gain)).astype(BF)

    def to_whole(plain):
        parts = token_gather(plain.reshape(seqs, quarter, width))
        whole = jnp.zeros((seqs, rows, width), BF)
        for k in range(4):
            whole = lax.dynamic_update_slice_in_dim(whole, parts[:, k], starts[k], 1)
        return whole

    d_down, grad_ffn_out = rms_back(down_sum, ffn_out_gain, upstream)
    d_down = wide_gather(d_down.astype(BF)).reshape(2 * tokens, width)
    d_hidden = dot("td,df->tf", d_down, full_down)
    gate_up, d_hidden = lax.optimization_barrier((gate_up, d_hidden))
    unused_hidden, geglu_back = jax.vjp(geglu, gate_up)
    d_gateup = geglu_back(d_hidden)[0].astype(BF)
    parts = dot("tf,df->td", d_gateup, full_gateup).reshape(8, own, width)
    parts = parts[:4].astype(F32) + flip(parts[4:].astype(BF), "core").astype(F32)
    low, ffn_in, d_gateup, d_down, hidden = lax.optimization_barrier(
        (parts.astype(BF), ffn_in, d_gateup, d_down, hidden)
    )
    ffn_term = jnp.concatenate(
        [dot("td,tf->df", ffn_in, d_gateup).astype(BF), dot("td,tf->df", d_down, hidden).astype(BF)],
        axis=1,
    )
    got = [shift(low[1], DEPTH, -1), shift(low[2], DEPTH, 1), shift(low[3], DEPTH, 2)]
    got, ffn_term = lax.optimization_barrier((got, ffn_term))
    d_ffn = parts[0] + got[0].astype(F32) + got[1].astype(F32) + got[2].astype(F32)
    ffn_rows = lax.psum_scatter(ffn_term, ("x", "y"), scatter_dimension=0, tiled=True)
    d_middle, grad_ffn_in = rms_back(middle, ffn_in_gain, d_ffn)
    d_middle = upstream + d_middle
    d_projected, grad_attn_out = rms_back(projected, attn_out_gain, d_middle)
    d_projected = dot("te,ed->td", d_projected.astype(BF), to_round).astype(BF)
    d_projected = token_gather(d_projected.reshape(seqs, quarter, width)).reshape(tokens, width)
    d_attended = dot("td,dh->th", d_projected, full_output).astype(BF)
    d_queries, d_keyval = attention_back(
        sequence_queries,
        keys_all,
        query_index.reshape(rows, 1),
        first_key,
        key_index.reshape(1, -1),
        scale,
        lse,
        d_attended.reshape(seqs, rows, head),
    )
    d_queries = d_queries.reshape(tokens, head)
    d_own = d_keyval[:, 2 * reach :].reshape(seqs, 1, 4, quarter, 2 * head)
    grid = (seqs, BACK, 2, quarter, 2 * head)
    d_got, d_other = d_keyval[:, :reach].reshape(grid), d_keyval[:, reach : 2 * reach].reshape(grid)
    got = flip(jnp.concatenate([d_other, d_own[:, :, 1::2]], axis=1), "core")
    halves = jnp.concatenate([d_got, d_own[:, :, 0::2]], axis=1).astype(F32) + got.astype(F32)
    terms = [
        lax.ppermute(
            halves[:, BACK - back].astype(BF),
            ("zh", "y"),
            [(i + back, i) for i in range(8 - back)],
        )
        for back in range(1, BACK + 1)
    ]
    terms[0], d_queries, d_projected = lax.optimization_barrier(
        (terms[0], d_queries, d_projected)
    )

    def query_path(raw_rows, gain):
        return rotate(rms_norm(raw_rows, gain), cosine, sine)

    def key_path(raw_rows, gain):
        return rotate(rms_norm(raw_rows, gain), own_of(cosine), own_of(sine))

    unused_query, query_back = jax.vjp(query_path, query_raw, query_gain)
    d_query_raw, grad_query = query_back(d_queries)
    d_query_raw = d_query_raw.astype(BF)
    query_term = dot("td,th->dh", normed, d_query_raw).astype(BF)
    output_term = dot("td,th->dh", d_projected, attended).astype(BF)
    narrow_term = jnp.concatenate([query_term, output_term], axis=1)
    narrow_term = narrow_term.reshape(4, 4, 2 * row_piece, 2 * head)
    along_x = [
        shift(narrow_term[:, 1], "x", -1),
        shift(narrow_term[:, 2], "x", 1),
        shift(narrow_term[:, 3], "x", 2),
    ]
    half = halves[:, BACK]
    for term in terms:
        half = half + term.astype(F32)
    d_keyval = half[:, 0] + flip(half[:, 1].astype(BF), "zl").astype(F32)
    d_keyval = d_keyval.reshape(own, 2 * head)
    d_keyval, along_x, d_middle = lax.optimization_barrier((d_keyval, along_x, d_middle))
    line = sum((value.astype(F32) for value in along_x), narrow_term[:, 0].astype(F32)).astype(BF)
    along_y = [shift(line[1], "y", -1), shift(line[2], "y", 1), shift(line[3], "y", 2)]
    d_normed_query = dot("th,dh->td", d_query_raw, full_query)
    d_normed = token_scatter(d_normed_query.reshape(seqs, 4, quarter, width)).reshape(own, width)
    unused_key, key_back = jax.vjp(key_path, own_of(key_raw), key_gain)
    d_key_raw, grad_key = key_back(d_keyval[:, :head])
    d_keyval_raw = jnp.concatenate([d_key_raw, d_keyval[:, head:]], axis=1).astype(BF)
    columns = 2 * head // 4
    parts = [
        lax.dynamic_slice_in_dim(d_keyval_raw, (member ^ k) * columns, columns, 1)
        for k in range(4)
    ]
    got = flip(jnp.stack([parts[1], parts[3]]), "core")
    over, along_y = lax.optimization_barrier(
        (flip(jnp.stack([parts[2], got[1]]), "zl"), along_y)
    )
    narrow_rows = sum((value.astype(F32) for value in along_y), line[0].astype(F32))
    column_parts = [parts[0], got[0], over[0], over[1]]
    column_rows = jnp.stack([v.reshape(seqs, quarter, columns) for v in column_parts], axis=1)
    keyval_term = dot("td,tk->dk", normed, column_rows.reshape(tokens, columns)).astype(BF)
    d_normed_keyval = dot("tk,dk->td", d_keyval_raw, full_keyval)
    inverse = inverse_rms(inputs)
    round_inputs = own_of(inputs)
    grad_attn_in = jnp.sum(d_normed_query * inputs * inverse, axis=0) + jnp.sum(
        d_normed_keyval * round_inputs * own_of(inverse), axis=0
    )
    wide = jnp.stack([grad_attn_out, grad_ffn_in, grad_ffn_out]).astype(BF)
    total = jnp.concatenate(
        [
            dot("ge,de->gd", grad_attn_in.astype(BF).reshape(1, -1), round_order).reshape(-1),
            dot("ge,de->gd", wide, straight).reshape(-1),
            grad_query,
            grad_key,
        ]
    )
    total = total.astype(BF).reshape(128, gain_piece)
    total = dot("ar,ag->rg", holder, jnp.pad(total, ((0, 0), (0, columns - gain_piece))))
    terms = jnp.concatenate(
        [keyval_term.reshape(16, -1, columns), total.astype(BF).reshape(16, 8, columns)], axis=1
    )
    terms, ffn_rows = lax.optimization_barrier((terms, ffn_rows))
    got = [
        shift(terms[4:8], "y", -1), shift(terms[8:12], "y", 1), shift(terms[12:], "y", 2)
    ]
    got[0], own_output, d_normed = lax.optimization_barrier((got[0], own_output, d_normed))
    terms = sum((value.astype(F32) for value in got), terms[:4].astype(F32)).astype(BF)
    terms = ring_scatter([terms[i] for i in range(4)], "x")
    d_inputs, unused_gain = rms_back(round_inputs, attn_in_gain, d_normed + d_normed_keyval)
    input_grad = dot("te,de->td", d_middle.astype(BF), straight) + dot(
        "te,de->td", d_inputs.astype(BF), round_order
    )
    input_grad = to_whole(input_grad.astype(BF)).astype(F32)
    block_output = to_whole(dot("te,de->td", own_output, straight).astype(BF))
    narrow_low = narrow_rows.astype(BF)
    over = flip(jnp.where(zh_at == 0, ffn_rows[row_piece:], ffn_rows[:row_piece]), "zh")
    narrow_low = narrow_rows.astype(BF)
    narrow_over = flip(
        jnp.where(zh_at == 0, narrow_low[row_piece:], narrow_low[:row_piece]), "zh"
    )
    mine = jnp.where(zh_at == 0, ffn_rows[:row_piece], ffn_rows[row_piece:])
    both = by_bit(zh_at, mine, over).astype(F32)
    gate_grad, up_grad, down_grad = (
        jnp.concatenate(
            [both[i][:, lanes * j : lanes * j + half_units] for i in range(2)], axis=1
        )
        for j in range(3)
    )
    gateup_grad = jnp.stack([gate_grad, up_grad], axis=1)
    down_grad = down_grad.T
    mine = jnp.where(zh_at == 0, narrow_rows[:row_piece], narrow_rows[row_piece:])
    narrow_grad = mine + narrow_over.astype(F32)
    query_grad = narrow_grad[:, :head]
    output_grad = narrow_grad[:, head:].T
    query_results = adam_step(query_weight, query_grad, query_first, query_second, True)
    output_results = adam_step(output_weight, output_grad, output_first, output_second, True)
    gateup_results = adam_step(gateup_weight, gateup_grad, gateup_first, gateup_second, True)
    down_results = adam_step(down_weight, down_grad, down_first, down_second, True)
    terms, gateup_results, down_results = lax.optimization_barrier(
        (terms, gateup_results, down_results)
    )
    keyval_part = terms[: 2 * row_piece].reshape(2, 4, part, columns)
    gain_part = terms[2 * row_piece :].reshape(2, 4, 1, columns)
    both = jnp.concatenate([keyval_part, gain_part], axis=2)
    mine = jnp.where(zh_at == 0, both[0], both[1])
    theirs = jnp.where(zh_at == 0, both[1], both[0]).astype(BF)
    mine = mine + flip(theirs, "zh").astype(F32)
    owners = exchange(
        [lax.dynamic_index_in_dim(mine, member ^ k, 0, keepdims=False) for k in range(4)]
    )
    keyval_grad = jnp.zeros((part, 2 * head), F32)
    gains_grad = jnp.zeros((gain_piece,), F32)
    for k in range(4):
        keyval_grad = lax.dynamic_update_slice_in_dim(
            keyval_grad, owners[k][:part], (member ^ k) * columns, 1
        )
        gains_grad = gains_grad + owners[k][part, :gain_piece]

    results = [block_output, input_grad]
    results.extend(query_results)
    results.extend(adam_step(keyval_weight, keyval_grad, keyval_first, keyval_second, True))
    results.extend(output_results)
    results.extend(gateup_results)
    results.extend(down_results)
    results.extend(adam_step(norm_gains, gains_grad, gains_first, gains_second, False))
    return tuple(results)


def solution(mesh):
    fine = Mesh(mesh.devices.reshape(4, 2, 4, 2, 2), ("x", "zh", "y", "zl", "core"))
    context = ("zh", "y")
    tensor = ("zl", "core")
    fsdp = ("x", "zh", "y")
    everything = fsdp + tensor
    stream = P("x", context, None)
    query = P(fsdp, tensor)
    keyval = P(everything, None)
    output = P(tensor, fsdp)
    gateup = P(fsdp, None, tensor)
    gains = P(everything)
    return jax.shard_map(
        shards,
        mesh=fine,
        in_specs=(
            stream, P("x", context), stream,
            query, keyval, output, gateup, output, gains,
            query, query, keyval, keyval, output, output,
            gateup, gateup, output, output, gains, gains,
        ),
        out_specs=(stream, stream)
        + (query,) * 4
        + (keyval,) * 4
        + (output,) * 4
        + (gateup,) * 4
        + (output,) * 4
        + (gains,) * 4,
        check_vma=False,
    )
```

```python
import jax
import jax.numpy as jnp
from jax import lax
from jax.experimental import pallas as pl
from jax.experimental.pallas import tpu as pltpu
from jax.sharding import Mesh
from jax.sharding import PartitionSpec as P

STEP = 4
EPSILON = 1e-06
ROPE_BASE = 1000000.0
LEARN_RATE = 0.02
GAIN_RATE = 0.5
WEIGHT_DECAY = 0.1
BETA_ONE = 0.5
BETA_TWO = 0.5
ADAM_EPS = 1e-08
MASKED = -1e30
BACK = 4

BF = jnp.bfloat16
F32 = jnp.float32


def dot(spec, left, right):
    return jnp.einsum(spec, left, right, preferred_element_type=F32)


def shift(value, axis, step):
    size = 4 if isinstance(axis, tuple) else lax.axis_size(axis)
    return lax.ppermute(value, axis, [(i, (i + step) % size) for i in range(size)])


def flip(value, axis):
    return shift(value, axis, 1)


def ring_gather(value, axis):
    return [value, shift(value, axis, 1), shift(value, axis, -1), shift(value, axis, 2)]


def ring_scatter(parts, axis):
    got = [shift(parts[1], axis, -1), shift(parts[2], axis, 1), shift(parts[3], axis, 2)]
    return parts[0].astype(F32) + got[0].astype(F32) + got[1].astype(F32) + got[2].astype(F32)


def by_bit(bit, mine, theirs):
    first = jnp.where(bit == 0, mine, theirs)
    return jnp.stack([first, jnp.where(bit == 0, theirs, mine)])


DEPTH = ("zh", "zl")


def wide_gather(own):
    four = jnp.stack(ring_gather(own, DEPTH))
    return jnp.concatenate([four, flip(four, "core")])


def wide_scatter(parts):
    got = flip(parts[4:].astype(BF), "core")
    four = parts[:4].astype(F32) + got.astype(F32)
    low = four.astype(BF)
    return ring_scatter([four[0], low[1], low[2], low[3]], DEPTH)


def token_gather(own):
    two = jnp.stack([own, flip(own, "zl")], axis=1)
    other = flip(two, "core")
    return jnp.stack([two[:, 0], other[:, 0], two[:, 1], other[:, 1]], axis=1)


def token_scatter(parts):
    got = flip(parts[:, 1::2].astype(BF), "core").astype(F32)
    mine = parts[:, 0].astype(F32) + got[:, 0]
    theirs = (parts[:, 2].astype(F32) + got[:, 1]).astype(BF)
    return mine + flip(theirs, "zl").astype(F32)


def exchange(parts):
    got = flip(jnp.stack([parts[1], parts[3]]), "core")
    over = flip(jnp.stack([parts[2], got[1]]), "zl")
    return [parts[0], got[0], over[0], over[1]]


def inverse_rms(vector):
    return lax.rsqrt(jnp.mean(vector * vector, axis=-1, keepdims=True) + EPSILON)


def rms_norm(vector, gain):
    return vector * inverse_rms(vector) * gain


def rms_back(vector, gain, upstream):
    inverse = inverse_rms(vector)
    scaled = upstream * gain
    inner = jnp.mean(scaled * vector, axis=-1, keepdims=True)
    return (
        inverse * (scaled - vector * (inverse * inverse) * inner),
        jnp.sum(upstream * vector * inverse, axis=0),
    )


def rotation(positions, head_size):
    half_size = head_size // 2
    inverse = jnp.exp(
        jnp.arange(half_size, dtype=F32) * (-2.0 * jnp.log(ROPE_BASE) / head_size)
    )
    angles = positions.astype(F32)[..., None] * inverse
    return jnp.cos(angles), jnp.sin(angles)


def rotate(vector, cosine, sine):
    half_size = vector.shape[-1] // 2
    first_half = vector[..., :half_size]
    second_half = vector[..., half_size:]
    return jnp.concatenate(
        [first_half * cosine - second_half * sine, second_half * cosine + first_half * sine],
        axis=-1,
    )


def adam_step(weight, gradient, first_old, second_old, decayed):
    weight_full = weight.astype(F32)
    first_new = BETA_ONE * first_old + (1.0 - BETA_ONE) * gradient
    second_new = BETA_TWO * second_old + (1.0 - BETA_TWO) * gradient * gradient
    first_hat = first_new / (1.0 - BETA_ONE**STEP)
    second_hat = second_new / (1.0 - BETA_TWO**STEP)
    change = first_hat / (jnp.sqrt(second_hat) + ADAM_EPS)
    if decayed:
        change = change + WEIGHT_DECAY * weight_full
        rate = LEARN_RATE
    else:
        rate = GAIN_RATE
    return (gradient, first_new, second_new, weight_full - rate * change)


def ring_place(index, slot):
    offset = jnp.where(slot == 0, 0, jnp.where(slot == 1, 3, jnp.where(slot == 2, 1, 2)))
    return (index + offset) % 4


def attention(queries, keyval, visible, scale):
    head = queries.shape[-1]
    scores = dot("sqh,skh->sqk", queries, keyval[..., :head]) * scale
    scores = jnp.where(visible, scores, MASKED)
    top = jnp.max(scores, axis=-1, keepdims=True)
    lse = top + jnp.log(jnp.sum(jnp.exp(scores - top), axis=-1, keepdims=True))
    probs = jnp.exp(scores - lse)
    return dot("sqk,skh->sqh", probs.astype(BF), keyval[..., head:]).astype(BF), lse


def tile_dot(left, right, left_dim, right_dim):
    return lax.dot_general(
        left, right, (((left_dim,), (right_dim,)), ((), ())), preferred_element_type=F32
    )


def attention_back_kernel(
    scale, queries, keyval, at, first, key_at, lse, upstream, d_queries, d_keyval
):
    head = queries.shape[-1]
    keys, values = keyval[0, :, :head], keyval[0, :, head:]
    rows, grads = queries[0], upstream[0]
    place = key_at[...]
    visible = (place <= at[...]) & (place >= first[0])
    scores = tile_dot(rows, keys, 1, 1) * scale
    probs = jnp.exp(jnp.where(visible, scores, MASKED) - lse[0])
    d_probs = tile_dot(grads, values, 1, 1)
    inner = jnp.sum(d_probs * probs, axis=-1, keepdims=True)
    d_scores = (probs * (d_probs - inner)).astype(BF)
    d_queries[0] = tile_dot(d_scores, keys, 1, 0) * scale
    d_keyval[0, :, :head] = (tile_dot(d_scores, rows, 0, 0) * scale).astype(BF)
    d_keyval[0, :, head:] = tile_dot(probs.astype(BF), grads, 0, 0).astype(BF)


def attention_back(queries, keyval, at, first, key_at, scale, lse, upstream):
    seqs, rows, head = queries.shape
    keys = keyval.shape[1]

    def kernel(*refs):
        attention_back_kernel(scale, *refs)

    def block(*shape):
        return pl.BlockSpec((1,) + shape, lambda i: (i, 0, 0))

    return pl.pallas_call(
        kernel,
        grid=(seqs,),
        in_specs=[
            block(rows, head),
            block(keys, 2 * head),
            pl.BlockSpec((rows, 1), lambda i: (0, 0)),
            block(rows, 1),
            pl.BlockSpec((1, keys), lambda i: (0, 0)),
            block(rows, 1),
            block(rows, head),
        ],
        out_specs=[block(rows, head), block(keys, 2 * head)],
        out_shape=[
            jax.ShapeDtypeStruct((seqs, rows, head), F32),
            jax.ShapeDtypeStruct((seqs, keys, 2 * head), BF),
        ],
        compiler_params=pltpu.CompilerParams(vmem_limit_bytes=40 * 1024 * 1024),
        cost_estimate=pl.CostEstimate(
            flops=10 * seqs * rows * keys * head,
            bytes_accessed=8 * seqs * keys * head,
            transcendentals=seqs * rows * keys,
        ),
    )(queries, keyval, at, first, key_at, lse, upstream)


def shards(
    block_input,
    positions,
    cotangent,
    query_weight,
    keyval_weight,
    output_weight,
    gateup_weight,
    down_weight,
    norm_gains,
    query_first,
    query_second,
    keyval_first,
    keyval_second,
    output_first,
    output_second,
    gateup_first,
    gateup_second,
    down_first,
    down_second,
    gains_first,
    gains_second,
):
    seqs, rows, width = block_input.shape
    head = keyval_weight.shape[1] // 2
    quarter = rows // 4
    own = seqs * quarter
    tokens = 4 * own
    scale = head ** (-0.5)
    x_at, zh_at, y_at, zl_at, core_at = (
        lax.axis_index(axis) for axis in ("x", "zh", "y", "zl", "core")
    )
    member = zl_at * 2 + core_at
    context_at = zh_at * 4 + y_at
    row_piece = query_weight.shape[0]

    part = keyval_weight.shape[0]
    gain_piece = norm_gains.shape[0]
    pad = 2 * head - gain_piece
    piece = jnp.concatenate([keyval_weight, jnp.pad(norm_gains, (0, pad)).reshape(1, -1)])
    piece = by_bit(core_at, piece, flip(piece, "core"))
    piece = by_bit(zl_at, piece, flip(piece, "zl"))
    narrow = jnp.concatenate([query_weight, output_weight.T], axis=1)
    piece = jnp.concatenate([piece.reshape(4 * (part + 1), 2 * head), narrow])
    piece, gateup_ready, down_ready = lax.optimization_barrier(
        (by_bit(zh_at, piece, flip(piece, "zh")), gateup_weight, down_weight)
    )
    narrow_rows = piece[:, 4 * (part + 1) :].reshape(2 * row_piece, 2 * head)
    piece = piece[:, : 4 * (part + 1)].reshape(8, part + 1, 2 * head)
    keyval_rows = piece[:, :part].reshape(8 * part, 2 * head)
    small = lax.optimization_barrier(jnp.concatenate([narrow_rows, piece[:, part]]))
    keyval_rows = lax.optimization_barrier(keyval_rows)
    line = jnp.concatenate(ring_gather(small, "x"))
    keyval_line = jnp.concatenate(ring_gather(keyval_rows, "y"))
    line, keyval_line = lax.optimization_barrier((line, keyval_line))
    small = jnp.concatenate(ring_gather(line, "y")).reshape(16, -1, 2 * head)
    lines = ring_gather(keyval_line, "x")
    lines[1], block_input, positions, x_at = lax.optimization_barrier(
        (lines[1], block_input, positions, x_at)
    )
    full_keyval = jnp.stack(lines).reshape(4, 4, 2 * row_piece, -1)
    full_keyval = full_keyval.transpose(1, 0, 2, 3).reshape(width, 2 * head)
    units = down_weight.shape[0]
    half_units = units // 2
    lanes = -(-half_units // 128) * 128
    fill = ((0, 0), (0, lanes - half_units))
    wide_parts = (gateup_ready[:, 0], gateup_ready[:, 1], down_ready.T)
    lower = jnp.concatenate([jnp.pad(w[:, :half_units], fill) for w in wide_parts], axis=1)
    upper = jnp.concatenate([jnp.pad(w[:, half_units:], fill) for w in wide_parts], axis=1)
    keep = jnp.where(zh_at == 0, lower, upper)
    send = jnp.where(zh_at == 0, upper, lower)
    bundle = by_bit(zh_at, keep, flip(send, "zh")).reshape(2 * row_piece, -1)
    bundle, small, full_keyval = lax.optimization_barrier((bundle, small, full_keyval))
    big = lax.all_gather(bundle, ("x", "y"), axis=0, tiled=True)
    full_query = small[:, : 2 * row_piece, :head].reshape(width, head)
    full_output = small[:, : 2 * row_piece, head:].reshape(width, head)
    place = lax.broadcasted_iota(jnp.int32, (width, width), 1)
    source_row = lax.broadcasted_iota(jnp.int32, (width, width), 0)
    group = place // (2 * row_piece)
    inner_row = ((place // row_piece) % 2) * 4 * row_piece + place % row_piece
    straight = (source_row == inner_row + ((group // 4) * 8 + group % 4) * row_piece).astype(BF)
    round_x, round_y = ring_place(x_at, group % 4), ring_place(y_at, group // 4)
    round_block, source_block = round_x * 8 + round_y, round_x * 4 + round_y
    round_order = (source_row == inner_row + round_block * row_piece).astype(BF)
    to_round = (source_row == source_block * 2 * row_piece + place % (2 * row_piece)).astype(BF)

    slot = lax.broadcasted_iota(jnp.int32, (128, 128), 1)
    holder = (
        (ring_place(x_at, (slot // 8) % 4) * 2 + (slot // 4) % 2) * 4
        + ring_place(y_at, slot // 32)
    ) * 4 + slot % 4
    holder = (lax.broadcasted_iota(jnp.int32, (128, 128), 0) == holder).astype(BF)
    gain_rows = small[:, 2 * row_piece :, :128].reshape(128, 128)
    gains_all = dot("ar,rg->ag", holder, gain_rows)[:, :gain_piece].astype(BF).reshape(-1)
    model_gains = gains_all[: 4 * width].reshape(4, width)
    attn_in_gain = lax.optimization_barrier(dot("gd,de->ge", model_gains, round_order))[0]
    straight_gains = dot("gd,de->ge", model_gains, straight)
    attn_out_gain, ffn_in_gain, ffn_out_gain = (straight_gains[i] for i in range(1, 4))
    query_gain = gains_all[4 * width : 4 * width + head].astype(F32)
    key_gain = gains_all[4 * width + head :].astype(F32)

    starts = [(member ^ k) * quarter for k in range(4)]

    def quarters(array):
        return jnp.concatenate(
            [lax.dynamic_slice_in_dim(array, start, quarter, 1) for start in starts], axis=1
        )

    def own_of(array):
        return array.reshape(seqs, 4, quarter, -1)[:, 0].reshape(own, -1)

    token_rows = quarters(block_input).reshape(tokens, width)
    inputs = dot("td,de->te", token_rows, round_order)
    own_inputs = dot("td,de->te", own_of(token_rows), straight)
    own_cotangent = lax.dynamic_slice_in_dim(cotangent, starts[0], quarter, 1)
    upstream = dot("td,de->te", own_cotangent.reshape(own, width), straight)
    place_of = quarters(positions)
    cosine, sine = rotation(place_of.reshape(tokens), head)

    normed = rms_norm(inputs, attn_in_gain).astype(BF)
    query_raw = dot("td,dh->th", normed, full_query)
    raw = dot("td,dh->th", normed, full_keyval)
    key_raw, value_raw = raw[:, :head], raw[:, head:]
    queries = rotate(rms_norm(query_raw, query_gain), cosine, sine).astype(BF)
    key_rows = rotate(rms_norm(key_raw, key_gain), cosine, sine)
    keyval = jnp.concatenate([key_rows, value_raw], axis=1).astype(BF)
    keyval = keyval.reshape(seqs, 4, quarter, 2 * head)
    half = keyval[:, 0::2]
    got = jnp.stack(
        [
            lax.ppermute(half, ("zh", "y"), [(i, i + back) for i in range(8 - back)])
            for back in range(BACK, 0, -1)
        ],
        axis=1,
    )
    other = flip(got, "core")
    keys_all = jnp.concatenate(
        [array.reshape(seqs, -1, 2 * head) for array in (got, other, keyval)], axis=1
    )
    reach = BACK * rows // 2

    def position_of(block, place_in, row):
        return (context_at + block) * rows + (member ^ place_in) * quarter + row

    index = lax.broadcasted_iota(jnp.int32, (1, rows, 1), 1)
    query_index = position_of(0, index // quarter, index % quarter)
    index = lax.broadcasted_iota(jnp.int32, (1, 1, 2 * reach + rows), 2)
    before = index < 2 * reach
    block = jnp.where(before, (index % reach) // (rows // 2) - BACK, 0)
    slot = jnp.where(
        before, (index // quarter) % 2 * 2 + index // reach, (index - 2 * reach) // quarter
    )
    key_index = position_of(block, slot, index % quarter)
    first_key = query_index - place_of[:, :, None]
    visible = (key_index <= query_index) & (key_index >= first_key)

    sequence_queries = queries.reshape(seqs, rows, head)
    attended, lse = attention(sequence_queries, keys_all, visible, scale)
    attended = attended.reshape(tokens, head)
    projected = token_scatter(
        dot("th,dh->td", attended, full_output).reshape(seqs, 4, quarter, width)
    ).reshape(own, width)
    high = projected.astype(BF)
    both = jnp.concatenate([high, (projected - high.astype(F32)).astype(BF)])
    both = dot("te,de->td", both, to_round)
    projected = both[:own] + both[own:]
    middle = own_inputs + rms_norm(projected, attn_out_gain)
    ffn_own = rms_norm(middle, ffn_in_gain).astype(BF)
    four = ring_gather(ffn_own, DEPTH)
    four[1], big = lax.optimization_barrier((four[1], big))
    full_gateup, full_down = big[:, : 2 * lanes], big[:, 2 * lanes :]
    four = jnp.stack(four)
    ffn_in = jnp.concatenate([four, flip(four, "core")]).reshape(2 * tokens, width)
    gate_up = dot("td,df->tf", ffn_in, full_gateup)

    def geglu(pair):
        return jax.nn.gelu(pair[:, :lanes], approximate=True) * pair[:, lanes:]

    hidden = geglu(gate_up).astype(BF)
    down_sum = wide_scatter(dot("tf,df->td", hidden, full_down).reshape(8, own, width))
    own_output = (middle + rms_norm(down_sum, ffn_out_gain)).astype(BF)

    def to_whole(plain):
        parts = token_gather(plain.reshape(seqs, quarter, width))
        whole = jnp.zeros((seqs, rows, width), BF)
        for k in range(4):
            whole = lax.dynamic_update_slice_in_dim(whole, parts[:, k], starts[k], 1)
        return whole

    d_down, grad_ffn_out = rms_back(down_sum, ffn_out_gain, upstream)
    d_down = wide_gather(d_down.astype(BF)).reshape(2 * tokens, width)
    d_hidden = dot("td,df->tf", d_down, full_down)
    gate_up, d_hidden = lax.optimization_barrier((gate_up, d_hidden))
    unused_hidden, geglu_back = jax.vjp(geglu, gate_up)
    d_gateup = geglu_back(d_hidden)[0].astype(BF)
    parts = dot("tf,df->td", d_gateup, full_gateup).reshape(8, own, width)
    parts = parts[:4].astype(F32) + flip(parts[4:].astype(BF), "core").astype(F32)
    low, ffn_in, d_gateup, d_down, hidden = lax.optimization_barrier(
        (parts.astype(BF), ffn_in, d_gateup, d_down, hidden)
    )
    ffn_term = jnp.concatenate(
        [dot("td,tf->df", ffn_in, d_gateup).astype(BF), dot("td,tf->df", d_down, hidden).astype(BF)],
        axis=1,
    )
    got = [shift(low[1], DEPTH, -1), shift(low[2], DEPTH, 1), shift(low[3], DEPTH, 2)]
    got, ffn_term = lax.optimization_barrier((got, ffn_term))
    d_ffn = parts[0] + got[0].astype(F32) + got[1].astype(F32) + got[2].astype(F32)
    ffn_rows = lax.psum_scatter(ffn_term, ("x", "y"), scatter_dimension=0, tiled=True)
    d_middle, grad_ffn_in = rms_back(middle, ffn_in_gain, d_ffn)
    d_middle = upstream + d_middle
    d_projected, grad_attn_out = rms_back(projected, attn_out_gain, d_middle)
    d_projected = dot("te,ed->td", d_projected.astype(BF), to_round).astype(BF)
    d_projected = token_gather(d_projected.reshape(seqs, quarter, width)).reshape(tokens, width)
    d_attended = dot("td,dh->th", d_projected, full_output).astype(BF)
    d_queries, d_keyval = attention_back(
        sequence_queries,
        keys_all,
        query_index.reshape(rows, 1),
        first_key,
        key_index.reshape(1, -1),
        scale,
        lse,
        d_attended.reshape(seqs, rows, head),
    )
    d_queries = d_queries.reshape(tokens, head)
    d_own = d_keyval[:, 2 * reach :].reshape(seqs, 1, 4, quarter, 2 * head)
    grid = (seqs, BACK, 2, quarter, 2 * head)
    d_got, d_other = d_keyval[:, :reach].reshape(grid), d_keyval[:, reach : 2 * reach].reshape(grid)
    got = flip(jnp.concatenate([d_other, d_own[:, :, 1::2]], axis=1), "core")
    halves = jnp.concatenate([d_got, d_own[:, :, 0::2]], axis=1).astype(F32) + got.astype(F32)
    terms = [
        lax.ppermute(
            halves[:, BACK - back].astype(BF),
            ("zh", "y"),
            [(i + back, i) for i in range(8 - back)],
        )
        for back in range(1, BACK + 1)
    ]
    terms[0], d_queries, d_projected = lax.optimization_barrier(
        (terms[0], d_queries, d_projected)
    )

    def query_path(raw_rows, gain):
        return rotate(rms_norm(raw_rows, gain), cosine, sine)

    def key_path(raw_rows, gain):
        return rotate(rms_norm(raw_rows, gain), own_of(cosine), own_of(sine))

    unused_query, query_back = jax.vjp(query_path, query_raw, query_gain)
    d_query_raw, grad_query = query_back(d_queries)
    d_query_raw = d_query_raw.astype(BF)
    query_term = dot("td,th->dh", normed, d_query_raw).astype(BF)
    output_term = dot("td,th->dh", d_projected, attended).astype(BF)
    narrow_term = jnp.concatenate([query_term, output_term], axis=1)
    narrow_term = narrow_term.reshape(4, 4, 2 * row_piece, 2 * head)
    along_x = [
        shift(narrow_term[:, 1], "x", -1),
        shift(narrow_term[:, 2], "x", 1),
        shift(narrow_term[:, 3], "x", 2),
    ]
    half = halves[:, BACK]
    for term in terms:
        half = half + term.astype(F32)
    d_keyval = half[:, 0] + flip(half[:, 1].astype(BF), "zl").astype(F32)
    d_keyval = d_keyval.reshape(own, 2 * head)
    d_keyval, d_middle = lax.optimization_barrier((d_keyval, d_middle))
    d_normed_query = dot("th,dh->td", d_query_raw, full_query)
    d_normed = token_scatter(d_normed_query.reshape(seqs, 4, quarter, width)).reshape(own, width)
    unused_key, key_back = jax.vjp(key_path, own_of(key_raw), key_gain)
    d_key_raw, grad_key = key_back(d_keyval[:, :head])
    d_keyval_raw = jnp.concatenate([d_key_raw, d_keyval[:, head:]], axis=1).astype(BF)
    columns = 2 * head // 4
    parts = [
        lax.dynamic_slice_in_dim(d_keyval_raw, (member ^ k) * columns, columns, 1)
        for k in range(4)
    ]
    got = flip(jnp.stack([parts[1], parts[3]]), "core")
    got, along_x = lax.optimization_barrier((got, along_x))
    over = flip(jnp.stack([parts[2], got[1]]), "zl")
    line = sum((value.astype(F32) for value in along_x), narrow_term[:, 0].astype(F32)).astype(BF)
    along_y = [shift(line[1], "y", -1), shift(line[2], "y", 1), shift(line[3], "y", 2)]
    column_parts = [parts[0], got[0], over[0], over[1]]
    column_rows = jnp.stack([v.reshape(seqs, quarter, columns) for v in column_parts], axis=1)
    keyval_term = dot("td,tk->dk", normed, column_rows.reshape(tokens, columns)).astype(BF)
    d_normed_keyval = dot("tk,dk->td", d_keyval_raw, full_keyval)
    inverse = inverse_rms(inputs)
    round_inputs = own_of(inputs)
    grad_attn_in = jnp.sum(d_normed_query * inputs * inverse, axis=0) + jnp.sum(
        d_normed_keyval * round_inputs * own_of(inverse), axis=0
    )
    wide = jnp.stack([grad_attn_out, grad_ffn_in, grad_ffn_out]).astype(BF)
    total = jnp.concatenate(
        [
            dot("ge,de->gd", grad_attn_in.astype(BF).reshape(1, -1), round_order).reshape(-1),
            dot("ge,de->gd", wide, straight).reshape(-1),
            grad_query,
            grad_key,
        ]
    )
    total = total.astype(BF).reshape(128, gain_piece)
    total = dot("ar,ag->rg", holder, jnp.pad(total, ((0, 0), (0, columns - gain_piece))))
    terms = jnp.concatenate(
        [keyval_term.reshape(16, -1, columns), total.astype(BF).reshape(16, 8, columns)], axis=1
    )
    terms, ffn_rows = lax.optimization_barrier((terms, ffn_rows))
    got = [
        shift(terms[4:8], "y", -1), shift(terms[8:12], "y", 1), shift(terms[12:], "y", 2)
    ]
    got[0], own_output, d_normed, along_y = lax.optimization_barrier(
        (got[0], own_output, d_normed, along_y)
    )
    narrow_rows = sum((value.astype(F32) for value in along_y), line[0].astype(F32))
    terms = sum((value.astype(F32) for value in got), terms[:4].astype(F32)).astype(BF)
    terms = ring_scatter([terms[i] for i in range(4)], "x")
    d_inputs, unused_gain = rms_back(round_inputs, attn_in_gain, d_normed + d_normed_keyval)
    input_grad = dot("te,de->td", d_middle.astype(BF), straight) + dot(
        "te,de->td", d_inputs.astype(BF), round_order
    )
    input_grad = to_whole(input_grad.astype(BF)).astype(F32)
    block_output = to_whole(dot("te,de->td", own_output, straight).astype(BF))
    narrow_low = narrow_rows.astype(BF)
    over = flip(jnp.where(zh_at == 0, ffn_rows[row_piece:], ffn_rows[:row_piece]), "zh")
    narrow_low = narrow_rows.astype(BF)
    narrow_over = flip(
        jnp.where(zh_at == 0, narrow_low[row_piece:], narrow_low[:row_piece]), "zh"
    )
    mine = jnp.where(zh_at == 0, ffn_rows[:row_piece], ffn_rows[row_piece:])
    both = by_bit(zh_at, mine, over).astype(F32)
    gate_grad, up_grad, down_grad = (
        jnp.concatenate(
            [both[i][:, lanes * j : lanes * j + half_units] for i in range(2)], axis=1
        )
        for j in range(3)
    )
    gateup_grad = jnp.stack([gate_grad, up_grad], axis=1)
    down_grad = down_grad.T
    mine = jnp.where(zh_at == 0, narrow_rows[:row_piece], narrow_rows[row_piece:])
    narrow_grad = mine + narrow_over.astype(F32)
    query_grad = narrow_grad[:, :head]
    output_grad = narrow_grad[:, head:].T
    query_results = adam_step(query_weight, query_grad, query_first, query_second, True)
    output_results = adam_step(output_weight, output_grad, output_first, output_second, True)
    gateup_results = adam_step(gateup_weight, gateup_grad, gateup_first, gateup_second, True)
    down_results = adam_step(down_weight, down_grad, down_first, down_second, True)
    terms, gateup_results, down_results = lax.optimization_barrier(
        (terms, gateup_results, down_results)
    )
    keyval_part = terms[: 2 * row_piece].reshape(2, 4, part, columns)
    gain_part = terms[2 * row_piece :].reshape(2, 4, 1, columns)
    both = jnp.concatenate([keyval_part, gain_part], axis=2)
    mine = jnp.where(zh_at == 0, both[0], both[1])
    theirs = jnp.where(zh_at == 0, both[1], both[0]).astype(BF)
    mine = mine + flip(theirs, "zh").astype(F32)
    owners = exchange(
        [lax.dynamic_index_in_dim(mine, member ^ k, 0, keepdims=False) for k in range(4)]
    )
    keyval_grad = jnp.zeros((part, 2 * head), F32)
    gains_grad = jnp.zeros((gain_piece,), F32)
    for k in range(4):
        keyval_grad = lax.dynamic_update_slice_in_dim(
            keyval_grad, owners[k][:part], (member ^ k) * columns, 1
        )
        gains_grad = gains_grad + owners[k][part, :gain_piece]

    results = [block_output, input_grad]
    results.extend(query_results)
    results.extend(adam_step(keyval_weight, keyval_grad, keyval_first, keyval_second, True))
    results.extend(output_results)
    results.extend(gateup_results)
    results.extend(down_results)
    results.extend(adam_step(norm_gains, gains_grad, gains_first, gains_second, False))
    return tuple(results)


def solution(mesh):
    fine = Mesh(mesh.devices.reshape(4, 2, 4, 2, 2), ("x", "zh", "y", "zl", "core"))
    context = ("zh", "y")
    tensor = ("zl", "core")
    fsdp = ("x", "zh", "y")
    everything = fsdp + tensor
    stream = P("x", context, None)
    query = P(fsdp, tensor)
    keyval = P(everything, None)
    output = P(tensor, fsdp)
    gateup = P(fsdp, None, tensor)
    gains = P(everything)
    return jax.shard_map(
        shards,
        mesh=fine,
        in_specs=(
            stream, P("x", context), stream,
            query, keyval, output, gateup, output, gains,
            query, query, keyval, keyval, output, output,
            gateup, gateup, output, output, gains, gains,
        ),
        out_specs=(stream, stream)
        + (query,) * 4
        + (keyval,) * 4
        + (output,) * 4
        + (gateup,) * 4
        + (output,) * 4
        + (gains,) * 4,
        check_vma=False,
    )
```
